32 devices in a mesh: tm: 4 (over y, core), chan: 8 (over z, x).
Axes of the slice: x: 2, y: 2, z: 4, core: 2. Of those that a mesh axis runs over, the one named last changes fastest.
Arguments:
- strain: float32 [256, 16384], P('chan', 'tm'), may hold values from -16 to 16
- channel_mask: int32 [256], P('chan'), may hold values 0 or 1
Outputs:
- cleaned: float32 [256, 16384], P('chan', 'tm')
The draws below stay inside these ranges and needn't reach their ends.
All inputs are finite; a program needn't handle non-finite values. No bound on the sum of `channel_mask` on one device may be relied on, other than what follows from the above.
Results may differ from the reference program's by a relative error of at most 0.0003.
Values sent between devices are 32-bit elements; how exact they have to be, the bound alone decides.
No kernel may reach another device: no remote copies, remote signals or barrier semaphores. Data moves between devices by JAX's collectives and lax.ppermute only.
A program may use at most 64 MiB of HBM per device.

```python
import math
import jax
import jax.numpy as jnp
import numpy as np
from jax import lax

RADIUS = 16
NCH = 256
READING_COUNT = 16384


def draw_strain(key, part):
    subkeys = jax.random.split(key, 9)
    clock_readings = jnp.arange(READING_COUNT, dtype=jnp.float32)
    sinusoid_hertz = jnp.exp(jax.random.uniform(subkeys[0], (NCH, 1), jnp.float32, math.log(2e-05), math.log(0.0001)))
    sinusoid_angles = jax.random.uniform(subkeys[1], (NCH, 1), jnp.float32, -math.pi, math.pi)
    tone_steps = jax.random.randint(subkeys[6], (NCH, 1), 737, 1025).astype(jnp.int32)
    tone_clock = jnp.arange(READING_COUNT, dtype=jnp.int32)[None, :]
    tone_turns = (tone_clock * tone_steps % 4096).astype(jnp.float32) / 4096.0
    tone_angles = jax.random.uniform(subkeys[7], (NCH, 1), jnp.float32, -math.pi, math.pi)
    tone_wave = jnp.sin(2.0 * math.pi * tone_turns + tone_angles)
    gaussian_jitter = 0.5 * jnp.clip(jax.random.normal(subkeys[3], (NCH, READING_COUNT), jnp.float32), -6.0, 6.0)
    sensor_shifts = jax.random.uniform(subkeys[4], (NCH, 1), jnp.float32, -3.0, 3.0)
    oscillation_height = jax.random.uniform(subkeys[5], (NCH, 1), jnp.float32, 0.5, 2.0)
    tone_height = jax.random.uniform(subkeys[8], (NCH, 1), jnp.float32, 6.0, 8.0)
    slow_wave = oscillation_height * jnp.sin(2.0 * math.pi * sinusoid_hertz * clock_readings[None, :] + sinusoid_angles)
    return gaussian_jitter + sensor_shifts + slow_wave + tone_height * tone_wave


def set_ends(result, stream_key, low, top_value):
    dims = result.shape
    place = [jax.random.randint(jax.random.fold_in(stream_key, axis), (), 0, dims[axis]) for axis in range(len(dims))]
    result = result.at[tuple(place)].set(low)
    longest = dims.index(max(dims))
    place[longest] = (place[longest] + 1) % dims[longest]
    return result.at[tuple(place)].set(top_value)


def setup_inputs(seed: int = 0) -> dict:
    seeds = jax.random.split(jax.random.key(seed), 3)
    return {
        "strain": draw_strain(jax.random.fold_in(seeds[2], 71), 0),
        "channel_mask": set_ends((jax.random.randint(seeds[1], (NCH,), 0, 8) < 7).astype(jnp.int32), jax.random.fold_in(seeds[1], 1), 0, 1),
    }


low_corner = 0.015
high_corner = 100.0
sample_rate = 500.0
highest = lax.Precision.HIGHEST

def section(corner, highpass):
    warped = 2.0 * sample_rate * math.tan(math.pi * corner / sample_rate)
    scaled = warped / (2.0 * sample_rate * math.sqrt(2.0))
    numer_real = 1.0 - scaled
    numer_imag = scaled
    denom_real = 1.0 + scaled
    denom_imag = -scaled
    modulus = denom_real * denom_real + denom_imag * denom_imag
    pole_real = (numer_real * denom_real + numer_imag * denom_imag) / modulus
    pole_imag = (numer_imag * denom_real - numer_real * denom_imag) / modulus
    pole_norm = pole_real * pole_real + pole_imag * pole_imag
    zero_place = 1.0 if highpass else -1.0
    section_gain = ((1.0 + zero_place * pole_real) ** 2 + pole_imag * pole_imag) / 4.0
    linear = section_gain * (2.0 * pole_real - 2.0 * zero_place)
    constant = section_gain * (1.0 - pole_norm)
    shrink = 1.0 - math.sqrt(pole_norm)
    first_out = linear / shrink
    second = (constant + pole_real * linear) / (pole_imag * shrink)
    rotation = np.array([[pole_real, -pole_imag], [pole_imag, pole_real]])
    inject = np.array([shrink, 0.0])
    return (rotation, inject, np.array([first_out, second]), section_gain)

def filter_system():
    high_rotation, high_inject, high_out, high_gain = section(low_corner, True)
    low_rotation, low_inject, low_out, low_gain = section(high_corner, False)
    upper_rows = np.concatenate([high_rotation, np.zeros((2, 2))], axis=1)
    lower_rows = np.concatenate([np.outer(low_inject, high_out), low_rotation], axis=1)
    transition = np.concatenate([upper_rows, lower_rows], axis=0)
    driving = np.concatenate([high_inject, low_inject * high_gain])
    readout = np.concatenate([high_out * low_gain, low_out])
    direct = low_gain * high_gain
    return (transition, driving, readout, direct)

def spatial_taps(extent):
    positions = np.arange(-extent, extent + 1)
    window = 0.5 * (1.0 + np.cos(np.pi * positions / (extent + 1)))
    window = window / np.sum(window)
    return np.where(positions == 0, 1.0 - window, -window)

def run_filter(record):
    transition, driving, readout, direct = filter_system()
    transition = jnp.asarray(transition, jnp.float32)
    driving = jnp.asarray(driving, jnp.float32)
    readout = jnp.asarray(readout, jnp.float32)
    direct = jnp.asarray(direct, jnp.float32)

    def advance(current, column):
        output = jnp.dot(readout, current, precision=highest) + direct * column
        current = jnp.dot(transition, current, precision=highest) + driving[:, None] * column[None, :]
        return (current, output)
    initial = jnp.zeros((4, record.shape[0]), jnp.float32)
    unused, outputs = lax.scan(advance, initial, record.T)
    return outputs.T

def reference(strain, channel_mask):
    forward = run_filter(strain)
    backward = run_filter(forward[:, ::-1])[:, ::-1]
    masked = backward * channel_mask.astype(jnp.float32)[:, None]
    taps = spatial_taps(RADIUS)
    padded = jnp.pad(masked, ((RADIUS, RADIUS), (0, 0)))
    cleaned = jnp.zeros_like(masked)
    for offset_step in range(2 * RADIUS + 1):
        cleaned = cleaned + jnp.float32(taps[offset_step]) * padded[offset_step:offset_step + NCH]
    return cleaned
```

```python
import functools
import math

import jax
import jax.numpy as jnp
import numpy as np
from jax import lax
from jax.experimental import pallas as pl
from jax.experimental.pallas import tpu as pltpu
from jax.sharding import PartitionSpec as P

RADIUS = 16
BLOCK = 256
STATES = 8

low_corner = 0.015
high_corner = 100.0
sample_rate = 500.0
highest = lax.Precision.HIGHEST
VMEM = pltpu.VMEM
ANY = pl.ANY


def section(corner, highpass):
    warped = 2.0 * sample_rate * math.tan(math.pi * corner / sample_rate)
    scaled = warped / (2.0 * sample_rate * math.sqrt(2.0))
    numer_real = 1.0 - scaled
    denom_real = 1.0 + scaled
    denom_imag = -scaled
    modulus = denom_real * denom_real + denom_imag * denom_imag
    pole_real = (numer_real * denom_real + scaled * denom_imag) / modulus
    pole_imag = (scaled * denom_real - numer_real * denom_imag) / modulus
    pole_norm = pole_real * pole_real + pole_imag * pole_imag
    zero_place = 1.0 if highpass else -1.0
    section_gain = ((1.0 + zero_place * pole_real) ** 2 + pole_imag * pole_imag) / 4.0
    linear = section_gain * (2.0 * pole_real - 2.0 * zero_place)
    constant = section_gain * (1.0 - pole_norm)
    shrink = 1.0 - math.sqrt(pole_norm)
    first_out = linear / shrink
    second = (constant + pole_real * linear) / (pole_imag * shrink)
    rotation = np.array([[pole_real, -pole_imag], [pole_imag, pole_real]])
    inject = np.array([shrink, 0.0])
    return (rotation, inject, np.array([first_out, second]), section_gain)


def filter_system():
    high_rotation, high_inject, high_out, high_gain = section(low_corner, True)
    low_rotation, low_inject, low_out, low_gain = section(high_corner, False)
    upper_rows = np.concatenate([high_rotation, np.zeros((2, 2))], axis=1)
    lower_rows = np.concatenate([np.outer(low_inject, high_out), low_rotation], axis=1)
    transition = np.concatenate([upper_rows, lower_rows], axis=0)
    driving = np.concatenate([high_inject, low_inject * high_gain])
    readout = np.concatenate([high_out * low_gain, low_out])
    direct = low_gain * high_gain
    return (transition, driving, readout, direct)


def spatial_taps(extent):
    positions = np.arange(-extent, extent + 1)
    window = 0.5 * (1.0 + np.cos(np.pi * positions / (extent + 1)))
    window = window / np.sum(window)
    return np.where(positions == 0, 1.0 - window, -window)


def two_sided():
    transition, driving, readout, direct = filter_system()
    poles, vectors = np.linalg.eig(transition)
    gains = (readout @ vectors) * (np.linalg.inv(vectors) @ driving)
    pairs = 1.0 / (1.0 - poles[:, None] * poles[None, :])
    rho = direct * gains + gains * poles * (gains @ pairs)
    r0 = (direct * direct + gains @ pairs @ gains).real
    cut = -(gains / rho)[:, None] * pairs * gains[None, :]
    kept = [i for i in range(4) if poles[i].imag > 0]
    twin = [int(np.argmin(abs(poles - np.conj(poles[i])))) for i in kept]
    scale = 1.0 - abs(poles[kept])
    end = np.zeros((4, 4))
    for i, a in enumerate(kept):
        for j, (b, c) in enumerate(zip(kept, twin)):
            straight, crossed = cut[a, b], cut[a, c]
            of_real, of_imag = straight + crossed, 1j * (straight - crossed)
            ratio = scale[i] / scale[j]
            end[2 * i, 2 * j : 2 * j + 2] = of_real.real * ratio, of_imag.real * ratio
            end[2 * i + 1, 2 * j : 2 * j + 2] = of_real.imag * ratio, of_imag.imag * ratio
    return r0, rho[kept], poles[kept], scale, end


def power(poles, steps):
    out = np.zeros((4, 4))
    for i, p in enumerate(poles**steps):
        out[2 * i : 2 * i + 2, 2 * i : 2 * i + 2] = [[p.real, -p.imag], [p.imag, p.real]]
    return out


def time_tables(samples, parts):
    r0, rho, poles, scale, end = two_sided()
    blocks = samples // BLOCK
    lanes = blocks * STATES
    k = np.arange(BLOCK)
    r = np.concatenate([[r0], sum(2.0 * (c * p ** k[:-1]).real for c, p in zip(rho, poles))])
    toeplitz = r[abs(k[:, None] - k[None, :])]
    gather = np.zeros((BLOCK, STATES))
    spread = np.zeros((STATES, BLOCK))
    for i, (p, s, c) in enumerate(zip(poles, scale, rho)):
        for side, far, near in ((0, BLOCK - 1 - k, k), (4, k, BLOCK - 1 - k)):
            inject = s * p**far
            out = 2.0 * c / s * p**near
            gather[:, side + 2 * i] = inject.real
            gather[:, side + 2 * i + 1] = inject.imag
            spread[side + 2 * i] = out.real
            spread[side + 2 * i + 1] = -out.imag
    gather = np.tile(gather, (1, blocks))
    spread = np.tile(spread, (blocks, 1))
    step = [power(poles, BLOCK * m).T for m in range(blocks + 1)]
    inner = np.zeros((blocks, STATES, blocks, STATES))
    whole = np.zeros((blocks, STATES, STATES))
    carry = np.zeros((STATES, blocks, STATES))
    for b in range(blocks):
        for c in range(blocks):
            if c < b:
                inner[c, :4, b, :4] = step[b - c - 1]
            if c > b:
                inner[c, 4:, b, 4:] = step[c - b - 1]
        whole[b, :4, :4] = step[blocks - 1 - b]
        whole[b, 4:, 4:] = step[b]
        carry[:4, b, :4] = step[b]
        carry[4:, b, 4:] = step[blocks - 1 - b]
    inner = inner.reshape(lanes, lanes)
    whole = np.tile(whole.reshape(lanes, STATES), (1, blocks))
    carry = carry.reshape(STATES, lanes)
    device = [power(poles, samples * m).T for m in range(parts + 1)]
    enter = np.zeros((parts, lanes, lanes))
    for t in range(parts):
        for j in range(parts):
            at = (t - j) % parts
            into = np.zeros((STATES, STATES))
            if at < t:
                into[:4, :4] = device[t - at - 1]
            if at > t:
                into[4:, 4:] = device[at - t - 1]
            into[:4, 4:] = device[parts - 1 - at] @ end.T @ device[parts - 1 - t]
            enter[t, STATES * j : STATES * (j + 1)] = into @ carry
    return [np.asarray(v, np.float32) for v in (toeplitz, gather, spread, inner, whole, enter)]


def mix_tables(channels):
    taps = spatial_taps(RADIUS)

    def between(rows, columns):
        lag = columns[None, :] - rows[:, None]
        return np.where(abs(lag) <= RADIUS, taps[np.clip(lag + RADIUS, 0, 2 * RADIUS)], 0.0)

    mine = np.arange(channels)
    own = between(mine, mine)
    after = between(mine, channels + np.arange(RADIUS))
    before = between(mine, np.arange(-RADIUS, 0))
    both = [np.concatenate(v, axis=1) for v in ((own, after, before), (own, before, after))]
    return np.stack(both).astype(np.float32)


def halves(value):
    value = np.asarray(value, np.float32)
    high = value.astype(jnp.bfloat16)
    return high, (value - high.astype(np.float32)).astype(jnp.bfloat16)


def split(value):
    high = value.astype(jnp.bfloat16)
    return high, (value - high.astype(jnp.float32)).astype(jnp.bfloat16)


def exact(a, b):
    return jnp.dot(a, b, precision=highest, preferred_element_type=jnp.float32)


def product(a, b):
    return jnp.dot(a, b, preferred_element_type=jnp.float32)


def triple(a, high, low):
    a_high, a_low = split(a)
    return product(a_high, high) + (product(a_high, low) + product(a_low, high))


def triple_left(high, low, b):
    b_high, b_low = split(b)
    return product(high, b_high) + (product(low, b_high) + product(high, b_low))


def place():
    return lax.rem(lax.axis_index("chan"), 2)


def rows_of(x):
    return jnp.concatenate([x[:, i : i + BLOCK] for i in range(0, x.shape[1], BLOCK)], axis=0)


def keep_own(stacked, first, groups):
    rows = stacked.shape[0] // groups
    owner = lax.broadcasted_iota(jnp.int32, (rows, stacked.shape[1]), 1) // STATES
    return sum(
        jnp.where(owner == first + g, stacked[g * rows : (g + 1) * rows], 0.0)
        for g in range(groups)
    )


def spread_out(states, first, groups):
    owner = lax.broadcasted_iota(jnp.int32, states.shape, 1) // STATES
    return jnp.concatenate(
        [jnp.where(owner == first + g, states, 0.0) for g in range(groups)], axis=0
    )


def start_kernel(x_hbm, mask_hbm, gather_hbm, *refs):
    first1, second1, first2, second2, live, sums, x, mask, gather, sems = refs
    channels, samples = x.shape
    lanes = sums.shape[1]
    half = samples // 2
    parts = [pl.ds(0, half), pl.ds(half, half)]
    copies = [pltpu.make_async_copy(mask_hbm, mask, sems.at[0])]
    copies += [pltpu.make_async_copy(x_hbm.at[:, p], x.at[:, p], sems.at[1 + i]) for i, p in enumerate(parts)]
    copies += [pltpu.make_async_copy(gather_hbm, gather, sems.at[3])]
    for copy in copies:
        copy.start()
    odd = place()
    copies[0].wait()
    same = lax.broadcasted_iota(jnp.int32, (channels, channels), 0) == lax.broadcasted_iota(
        jnp.int32, (channels, channels), 1
    )
    alive = jnp.sum(
        jnp.where(same, mask[...].astype(jnp.float32), 0.0), axis=1, keepdims=True
    )
    total = jnp.zeros((channels, lanes), jnp.float32)
    for i, p in enumerate(parts):
        copies[1 + i].wait()
        here = x[:, p] * alive
        live[:, p] = here
        top, bottom = here[:RADIUS], here[channels - RADIUS :]
        to_first, to_second = jnp.where(odd == 1, top, bottom), jnp.where(odd == 1, bottom, top)
        if i == 0:
            first1[:, lanes:], second1[:, lanes:] = to_first, to_second
            copies[3].wait()
        else:
            first2[...], second2[...] = to_first, to_second
        high, low = split(rows_of(here))
        wide = product(high, gather[...])
        found = wide[:, :lanes] + wide[:, lanes:] + product(low, gather[:, :lanes])
        blocks = half // BLOCK
        total += keep_own(found, i * blocks, blocks)
    sums[...] = total
    top, bottom = total[:RADIUS], total[channels - RADIUS :]
    first1[:, :lanes] = jnp.where(odd == 1, top, bottom)
    second1[:, :lanes] = jnp.where(odd == 1, bottom, top)


def mixed_sums_kernel(sums, first1, second1, mix, out):
    lanes = sums.shape[1]
    stacked = jnp.concatenate([sums[...], first1[:, :lanes], second1[:, :lanes]], axis=0)
    out[...] = exact(mix[place()], stacked)


def early_kernel(live, first1, second1, mix, toeplitz, out):
    channels, samples = live.shape
    half = samples // 2
    lanes = first1.shape[1] - half
    high, low = split(mix[place()])
    for i in range(2):
        here = live[:, i * half : (i + 1) * half]
        if i == 0:
            here = jnp.concatenate([here, first1[:, lanes:], second1[:, lanes:]], axis=0)
            mixed = triple_left(high, low, here)
        else:
            mixed = triple_left(high[:, :channels], low[:, :channels], here)
        rows = triple(rows_of(mixed), toeplitz[:BLOCK], toeplitz[BLOCK:])
        for b in range(half // BLOCK):
            at = i * half + b * BLOCK
            out[:, at : at + BLOCK] = rows[b * channels : (b + 1) * channels]


def enter_kernel(parts, inner, whole, enter, *refs):
    sums, out = refs[:parts], refs[parts]
    stacked = jnp.concatenate([part[...] for part in sums], axis=0)
    totals = keep_own(exact(stacked, whole[...]), 0, parts)
    out[...] = exact(sums[0][...], inner[...]) + exact(totals, enter[lax.axis_index("tm")])


def finish_kernel(part, states, first2, second2, mix, toeplitz, spread, out_hbm, out, sems):
    channels, samples = part.shape
    lanes = states.shape[1]
    half = samples // 2
    blocks = half // BLOCK
    high, low = split(mix[place()][:, channels:])
    stores = []
    for i in range(2):
        rows = triple(spread_out(states[...], i * blocks, blocks), spread[:lanes], spread[lanes:])
        if i == 1:
            mixed = triple_left(high, low, jnp.concatenate([first2[...], second2[...]], axis=0))
            rows += triple(rows_of(mixed), toeplitz[:BLOCK], toeplitz[BLOCK:])
        for b in range(blocks):
            at = slice(i * half + b * BLOCK, i * half + (b + 1) * BLOCK)
            out[:, at] = part[:, at] + rows[b * channels : (b + 1) * channels]
        p = pl.ds(i * half, half)
        stores.append(pltpu.make_async_copy(out.at[:, p], out_hbm.at[:, p], sems.at[i]))
        stores[-1].start()
    for copy in stores:
        copy.wait()


def vmem(*shape, dtype=jnp.float32):
    return pltpu.VMEM(shape, dtype)


def kernel(body, name, inputs, outputs, scratch=(), cost=0, far=()):
    inputs = [
        pltpu.with_memory_space_constraint(v, pltpu.HBM if i in far else VMEM)
        for i, v in enumerate(inputs)
    ]
    out_specs = [
        pl.BlockSpec(memory_space=ANY if isinstance(o, jax.ShapeDtypeStruct) else VMEM)
        for o in outputs
    ]
    single = len(outputs) == 1
    return pl.pallas_call(
        body,
        out_shape=outputs[0] if single else tuple(outputs),
        in_specs=[pl.BlockSpec(memory_space=ANY if i in far else VMEM) for i in range(len(inputs))],
        out_specs=out_specs[0] if single else tuple(out_specs),
        scratch_shapes=list(scratch),
        compiler_params=pltpu.CompilerParams(vmem_limit_bytes=24 * 1024 * 1024),
        cost_estimate=pl.CostEstimate(flops=cost * 1000000000, bytes_accessed=0, transcendentals=0),
        name=name,
    )(*inputs)


def shards(strain, channel_mask):
    channels, samples = strain.shape
    parts = lax.axis_size("tm")
    places = lax.axis_size("chan")
    half = samples // 2
    lanes = samples // BLOCK * STATES
    toeplitz, gather, spread, inner, whole, enter = time_tables(samples, parts)
    gather = jnp.asarray(np.concatenate(halves(gather), axis=1))
    toeplitz = jnp.asarray(np.concatenate(halves(toeplitz), axis=0))
    spread = jnp.asarray(np.concatenate(halves(spread), axis=0))
    inner, whole, enter = map(jnp.asarray, (inner, whole, enter))
    mix = jnp.asarray(mix_tables(channels))

    pairs = [
        [(i + a, i + b) for i in range(start, places - 1, 2) for a, b in ((0, 1), (1, 0))]
        for start in (0, 1)
    ]
    first1, second1, first2, second2, live, sums = kernel(
        start_kernel,
        "start",
        [strain, channel_mask.reshape(1, channels), gather],
        [
            vmem(RADIUS, lanes + half),
            vmem(RADIUS, lanes + half),
            vmem(RADIUS, half),
            vmem(RADIUS, half),
            vmem(channels, samples),
            vmem(channels, lanes),
        ],
        [
            vmem(channels, samples),
            vmem(1, channels, dtype=jnp.int32),
            vmem(BLOCK, 2 * lanes, dtype=jnp.bfloat16),
            pltpu.SemaphoreType.DMA((4,)),
        ],
        far=(0, 1, 2),
    )
    first1 = lax.ppermute(first1, "chan", pairs[0])
    second1 = lax.ppermute(second1, "chan", pairs[1])
    first2 = lax.ppermute(first2, "chan", pairs[0])
    second2 = lax.ppermute(second2, "chan", pairs[1])
    sums = kernel(
        mixed_sums_kernel, "sums", [sums, first1, second1, mix], [vmem(channels, lanes)]
    )
    others = [
        lax.ppermute(sums, "tm", [(i, (i + j) % parts) for i in range(parts)])
        for j in range(1, parts)
    ]
    part = kernel(
        early_kernel, "early", [live, first1, second1, mix, toeplitz], [vmem(channels, samples)]
    )
    states = kernel(
        functools.partial(enter_kernel, parts),
        "enter",
        [inner, whole, enter, sums, *others],
        [vmem(channels, lanes)],
    )
    return kernel(
        finish_kernel,
        "finish",
        [part, states, first2, second2, mix, toeplitz, spread],
        [jax.ShapeDtypeStruct((channels, samples), jnp.float32)],
        [vmem(channels, samples), pltpu.SemaphoreType.DMA((2,))],
    )


def solution(mesh):
    placed = (P("chan", "tm"), P("chan"))
    return jax.shard_map(
        shards, mesh=mesh, in_specs=placed, out_specs=P("chan", "tm"), check_vma=False
    )
```

```python
import functools
import math

import jax
import jax.numpy as jnp
import numpy as np
from jax import lax
from jax.experimental import pallas as pl
from jax.experimental.pallas import tpu as pltpu
from jax.sharding import PartitionSpec as P

RADIUS = 16
BLOCK = 256
STATES = 8
SUMS_COST = 0

low_corner = 0.015
high_corner = 100.0
sample_rate = 500.0
highest = lax.Precision.HIGHEST
VMEM = pltpu.VMEM
ANY = pl.ANY


def section(corner, highpass):
    warped = 2.0 * sample_rate * math.tan(math.pi * corner / sample_rate)
    scaled = warped / (2.0 * sample_rate * math.sqrt(2.0))
    numer_real = 1.0 - scaled
    denom_real = 1.0 + scaled
    denom_imag = -scaled
    modulus = denom_real * denom_real + denom_imag * denom_imag
    pole_real = (numer_real * denom_real + scaled * denom_imag) / modulus
    pole_imag = (scaled * denom_real - numer_real * denom_imag) / modulus
    pole_norm = pole_real * pole_real + pole_imag * pole_imag
    zero_place = 1.0 if highpass else -1.0
    section_gain = ((1.0 + zero_place * pole_real) ** 2 + pole_imag * pole_imag) / 4.0
    linear = section_gain * (2.0 * pole_real - 2.0 * zero_place)
    constant = section_gain * (1.0 - pole_norm)
    shrink = 1.0 - math.sqrt(pole_norm)
    first_out = linear / shrink
    second = (constant + pole_real * linear) / (pole_imag * shrink)
    rotation = np.array([[pole_real, -pole_imag], [pole_imag, pole_real]])
    inject = np.array([shrink, 0.0])
    return (rotation, inject, np.array([first_out, second]), section_gain)


def filter_system():
    high_rotation, high_inject, high_out, high_gain = section(low_corner, True)
    low_rotation, low_inject, low_out, low_gain = section(high_corner, False)
    upper_rows = np.concatenate([high_rotation, np.zeros((2, 2))], axis=1)
    lower_rows = np.concatenate([np.outer(low_inject, high_out), low_rotation], axis=1)
    transition = np.concatenate([upper_rows, lower_rows], axis=0)
    driving = np.concatenate([high_inject, low_inject * high_gain])
    readout = np.concatenate([high_out * low_gain, low_out])
    direct = low_gain * high_gain
    return (transition, driving, readout, direct)


def spatial_taps(extent):
    positions = np.arange(-extent, extent + 1)
    window = 0.5 * (1.0 + np.cos(np.pi * positions / (extent + 1)))
    window = window / np.sum(window)
    return np.where(positions == 0, 1.0 - window, -window)


def two_sided():
    transition, driving, readout, direct = filter_system()
    poles, vectors = np.linalg.eig(transition)
    gains = (readout @ vectors) * (np.linalg.inv(vectors) @ driving)
    pairs = 1.0 / (1.0 - poles[:, None] * poles[None, :])
    rho = direct * gains + gains * poles * (gains @ pairs)
    r0 = (direct * direct + gains @ pairs @ gains).real
    cut = -(gains / rho)[:, None] * pairs * gains[None, :]
    kept = [i for i in range(4) if poles[i].imag > 0]
    twin = [int(np.argmin(abs(poles - np.conj(poles[i])))) for i in kept]
    scale = 1.0 - abs(poles[kept])
    end = np.zeros((4, 4))
    for i, a in enumerate(kept):
        for j, (b, c) in enumerate(zip(kept, twin)):
            straight, crossed = cut[a, b], cut[a, c]
            of_real, of_imag = straight + crossed, 1j * (straight - crossed)
            ratio = scale[i] / scale[j]
            end[2 * i, 2 * j : 2 * j + 2] = of_real.real * ratio, of_imag.real * ratio
            end[2 * i + 1, 2 * j : 2 * j + 2] = of_real.imag * ratio, of_imag.imag * ratio
    return r0, rho[kept], poles[kept], scale, end


def power(poles, steps):
    out = np.zeros((4, 4))
    for i, p in enumerate(poles**steps):
        out[2 * i : 2 * i + 2, 2 * i : 2 * i + 2] = [[p.real, -p.imag], [p.imag, p.real]]
    return out


def time_tables(samples, parts):
    r0, rho, poles, scale, end = two_sided()
    blocks = samples // BLOCK
    lanes = blocks * STATES
    k = np.arange(BLOCK)
    r = np.concatenate([[r0], sum(2.0 * (c * p ** k[:-1]).real for c, p in zip(rho, poles))])
    toeplitz = r[abs(k[:, None] - k[None, :])]
    gather = np.zeros((BLOCK, STATES))
    spread = np.zeros((STATES, BLOCK))
    for i, (p, s, c) in enumerate(zip(poles, scale, rho)):
        for side, far, near in ((0, BLOCK - 1 - k, k), (4, k, BLOCK - 1 - k)):
            inject = s * p**far
            out = 2.0 * c / s * p**near
            gather[:, side + 2 * i] = inject.real
            gather[:, side + 2 * i + 1] = inject.imag
            spread[side + 2 * i] = out.real
            spread[side + 2 * i + 1] = -out.imag
    gather = np.tile(gather, (1, blocks))
    spread = np.tile(spread, (blocks, 1))
    step = [power(poles, BLOCK * m).T for m in range(blocks + 1)]
    inner = np.zeros((blocks, STATES, blocks, STATES))
    whole = np.zeros((blocks, STATES, STATES))
    carry = np.zeros((STATES, blocks, STATES))
    for b in range(blocks):
        for c in range(blocks):
            if c < b:
                inner[c, :4, b, :4] = step[b - c - 1]
            if c > b:
                inner[c, 4:, b, 4:] = step[c - b - 1]
        whole[b, :4, :4] = step[blocks - 1 - b]
        whole[b, 4:, 4:] = step[b]
        carry[:4, b, :4] = step[b]
        carry[4:, b, 4:] = step[blocks - 1 - b]
    inner = inner.reshape(lanes, lanes)
    whole = whole.reshape(lanes, STATES).T
    carry = carry.reshape(STATES, lanes)
    device = [power(poles, samples * m).T for m in range(parts + 1)]
    enter = np.zeros((parts, parts * STATES, lanes))
    for t in range(parts):
        for j in range(parts):
            at = (t - j) % parts
            into = np.zeros((STATES, STATES))
            if at < t:
                into[:4, :4] = device[t - at - 1]
            if at > t:
                into[4:, 4:] = device[at - t - 1]
            into[:4, 4:] = device[parts - 1 - at] @ end.T @ device[parts - 1 - t]
            enter[t, STATES * j : STATES * (j + 1)] = into @ carry
    return [np.asarray(v, np.float32) for v in (toeplitz, gather, spread, inner, whole, enter)]


def mix_tables(channels):
    taps = spatial_taps(RADIUS)

    def between(rows, columns):
        lag = columns[None, :] - rows[:, None]
        return np.where(abs(lag) <= RADIUS, taps[np.clip(lag + RADIUS, 0, 2 * RADIUS)], 0.0)

    mine = np.arange(channels)
    own = between(mine, mine)
    after = between(mine, channels + np.arange(RADIUS))
    before = between(mine, np.arange(-RADIUS, 0))
    both = [np.concatenate(v, axis=1) for v in ((own, after, before), (own, before, after))]
    return np.stack(both).astype(np.float32)


def halves(value):
    value = np.asarray(value, np.float32)
    high = value.astype(jnp.bfloat16)
    return high, (value - high.astype(np.float32)).astype(jnp.bfloat16)


def split(value):
    high = value.astype(jnp.bfloat16)
    return high, (value - high.astype(jnp.float32)).astype(jnp.bfloat16)


def exact(a, b):
    return jnp.dot(a, b, precision=highest, preferred_element_type=jnp.float32)


def product(a, b):
    return jnp.dot(a, b, preferred_element_type=jnp.float32)


def mixing(weights, x):
    a, b = split(weights)
    high, low = split(x)
    return product(jnp.concatenate([a, b, a], axis=1), jnp.concatenate([high, high, low], axis=0))


def filtering(rows, toeplitz):
    high, low = split(rows)
    above, below = toeplitz[:BLOCK], toeplitz[BLOCK:]
    return product(
        jnp.concatenate([high, high, low], axis=1), jnp.concatenate([above, below, above], axis=0)
    )


def place():
    return lax.rem(lax.axis_index("chan"), 2)


def rows_of(x):
    return jnp.concatenate([x[:, i : i + BLOCK] for i in range(0, x.shape[1], BLOCK)], axis=0)


def keep_own(stacked, groups):
    rows = stacked.shape[0] // groups
    owner = lax.broadcasted_iota(jnp.int32, (rows, stacked.shape[1]), 1) // STATES
    return sum(
        jnp.where(owner == g, stacked[g * rows : (g + 1) * rows], 0.0) for g in range(groups)
    )


def spreading(states, first, groups, spread):
    lanes = states.shape[1]
    owner = lax.broadcasted_iota(jnp.int32, states.shape, 1) // STATES
    rows = [jnp.where(owner == first + g, states, 0.0) for g in range(groups)]
    high, low = split(jnp.concatenate(rows, axis=0))
    above, below = spread[:lanes], spread[lanes:]
    return product(
        jnp.concatenate([high, low], axis=1), jnp.concatenate([above, above], axis=0)
    ) + product(high, below)


def start_kernel(cuts, x_hbm, mask_hbm, gather_hbm, *refs):
    first1, second1, first2, second2, live, sums, x, mask, gather, sems = refs
    channels = x.shape[0]
    lanes = sums.shape[1]
    copies = [
        pltpu.make_async_copy(source, target, sems.at[i])
        for i, (source, target) in enumerate([(mask_hbm, mask), (gather_hbm, gather), (x_hbm, x)])
    ]
    for copy in copies:
        copy.start()
    odd = place()
    copies[0].wait()
    same = lax.broadcasted_iota(jnp.int32, (channels, channels), 0) == lax.broadcasted_iota(
        jnp.int32, (channels, channels), 1
    )
    alive = jnp.sum(
        jnp.where(same, mask[...].astype(jnp.float32), 0.0), axis=1, keepdims=True
    )
    copies[1].wait()
    copies[2].wait()
    here = x[...] * alive
    live[...] = here

    def send(value, first, second):
        top, bottom = value[:RADIUS], value[channels - RADIUS :]
        for out, even_rows, odd_rows in ((first, bottom, top), (second, top, bottom)):
            rows = jnp.where(odd == 1, odd_rows, even_rows)
            start = 0
            for ref, at, stop in out:
                if stop > start:
                    ref[:, at : at + stop - start] = rows[:, start:stop]
                start = stop

    samples = here.shape[1]
    send(
        here,
        [(first1, lanes, cuts[0]), (first2, 0, samples)],
        [(second1, lanes, cuts[1]), (second2, 0, samples)],
    )
    high, low = split(rows_of(here))
    wide = product(high, gather[...])
    found = wide[:, :lanes] + wide[:, lanes:] + product(low, gather[:, :lanes])
    total = keep_own(found, samples // BLOCK)
    sums[...] = total
    send(total, [(first1, 0, lanes)], [(second1, 0, lanes)])


def sums_kernel(sums, first1, second1, mix, whole, out, device_out):
    lanes = sums.shape[1]
    stacked = jnp.concatenate([sums[...], first1[:, :lanes], second1[:, :lanes]], axis=0)
    total = exact(mix[place()], stacked)
    out[...] = total
    device_out[...] = lax.dot_general(
        whole[...], total, (((1,), (1,)), ((), ())), precision=highest
    )


def padded(value, before, after):
    rows = value.shape[0]
    sides = [jnp.zeros((rows, n), jnp.float32) if n else None for n in (before, after)]
    return jnp.concatenate([v for v in (sides[0], value, sides[1]) if v is not None], axis=1)


def early_kernel(live, first1, second1, sums, mix, toeplitz, inner, out, states):
    channels, samples = live.shape
    lanes = sums.shape[1]
    states[...] = exact(sums[...], inner[...])
    edges = [padded(ref[:, lanes:], 0, samples + lanes - ref.shape[1]) for ref in (first1, second1)]
    mixed = mixing(mix[place()], jnp.concatenate([live[...], *edges], axis=0))
    rows = filtering(rows_of(mixed), toeplitz[...])
    for b in range(samples // BLOCK):
        out[:, b * BLOCK : (b + 1) * BLOCK] = rows[b * channels : (b + 1) * channels]


def finish_kernel(cuts, part, states, first2, second2, mix, toeplitz, enter, spread, *refs):
    devices, (out_hbm, out, sems) = refs[:-3], refs[-3:]
    channels, samples = part.shape
    cut = min(cuts)
    at = lax.axis_index("tm")
    arrived = jnp.concatenate([ref[...] for ref in devices], axis=0)
    inside = states[...] + lax.dot_general(
        arrived, enter[at], (((0,), (0,)), ((), ())), precision=highest
    )
    weights = mix[place()][:, channels:]
    stores = []
    for i, (start, stop) in enumerate(((0, cut), (cut, samples))):
        groups = (stop - start) // BLOCK
        rows = spreading(inside, start // BLOCK, groups, spread[...])
        if i == 1:
            edges = [padded(ref[...], stop - start - ref.shape[1], 0) for ref in (first2, second2)]
            mixed = mixing(weights, jnp.concatenate(edges, axis=0))
            rows += filtering(rows_of(mixed), toeplitz[...])
        for b in range(groups):
            here = slice(start + b * BLOCK, start + (b + 1) * BLOCK)
            out[:, here] = part[:, here] + rows[b * channels : (b + 1) * channels]
        p = pl.ds(start, stop - start)
        stores.append(pltpu.make_async_copy(out.at[:, p], out_hbm.at[:, p], sems.at[i]))
        stores[-1].start()
    for copy in stores:
        copy.wait()


def vmem(*shape, dtype=jnp.float32):
    return pltpu.VMEM(shape, dtype)


def kernel(body, name, inputs, outputs, scratch=(), cost=0, far=()):
    inputs = [
        pltpu.with_memory_space_constraint(v, pltpu.HBM if i in far else VMEM)
        for i, v in enumerate(inputs)
    ]
    out_specs = [
        pl.BlockSpec(memory_space=ANY if isinstance(o, jax.ShapeDtypeStruct) else VMEM)
        for o in outputs
    ]
    single = len(outputs) == 1
    return pl.pallas_call(
        body,
        out_shape=outputs[0] if single else tuple(outputs),
        in_specs=[pl.BlockSpec(memory_space=ANY if i in far else VMEM) for i in range(len(inputs))],
        out_specs=out_specs[0] if single else tuple(out_specs),
        scratch_shapes=list(scratch),
        compiler_params=pltpu.CompilerParams(vmem_limit_bytes=24 * 1024 * 1024),
        cost_estimate=pl.CostEstimate(flops=cost * 1000000000, bytes_accessed=0, transcendentals=0),
        name=name,
    )(*inputs)


def shards(strain, channel_mask):
    channels, samples = strain.shape
    parts = lax.axis_size("tm")
    places = lax.axis_size("chan")
    lanes = samples // BLOCK * STATES
    cuts = (samples // 2, samples // 2)
    toeplitz, gather, spread, inner, whole, enter = time_tables(samples, parts)
    gather = jnp.asarray(np.concatenate(halves(gather), axis=1))
    toeplitz = jnp.asarray(np.concatenate(halves(toeplitz), axis=0))
    spread = jnp.asarray(np.concatenate(halves(spread), axis=0))
    inner, whole, enter = map(jnp.asarray, (inner, whole, enter))
    mix = jnp.asarray(mix_tables(channels))

    pairs = [
        [(i + a, i + b) for i in range(start, places - 1, 2) for a, b in ((0, 1), (1, 0))]
        for start in (0, 1)
    ]
    first1, second1, first2, second2, live, sums = kernel(
        functools.partial(start_kernel, cuts),
        "start",
        [strain, channel_mask.reshape(1, channels), gather],
        [
            vmem(RADIUS, lanes + cuts[0]),
            vmem(RADIUS, lanes + cuts[1]),
            vmem(RADIUS, samples - cuts[0]),
            vmem(RADIUS, samples - cuts[1]),
            vmem(channels, samples),
            vmem(channels, lanes),
        ],
        [
            vmem(channels, samples),
            vmem(1, channels, dtype=jnp.int32),
            vmem(BLOCK, 2 * lanes, dtype=jnp.bfloat16),
            pltpu.SemaphoreType.DMA((3,)),
        ],
        far=(0, 1, 2),
    )
    first1 = lax.ppermute(first1, "chan", pairs[0])
    second1 = lax.ppermute(second1, "chan", pairs[1])
    first2 = lax.ppermute(first2, "chan", pairs[0])
    second2 = lax.ppermute(second2, "chan", pairs[1])
    sums, device = kernel(
        sums_kernel,
        "sums",
        [sums, first1, second1, mix, whole],
        [vmem(channels, lanes), vmem(STATES, channels)],
        cost=SUMS_COST,
    )
    others = [
        lax.ppermute(device, "tm", [(i, (i + j) % parts) for i in range(parts)])
        for j in range(1, parts)
    ]
    part, states = kernel(
        early_kernel,
        "early",
        [live, first1, second1, sums, mix, toeplitz, inner],
        [vmem(channels, samples), vmem(channels, lanes)],
    )
    return kernel(
        functools.partial(finish_kernel, cuts),
        "finish",
        [part, states, first2, second2, mix, toeplitz, enter, spread, device, *others],
        [jax.ShapeDtypeStruct((channels, samples), jnp.float32)],
        [vmem(channels, samples), pltpu.SemaphoreType.DMA((2,))],
    )


def solution(mesh):
    placed = (P("chan", "tm"), P("chan"))
    return jax.shard_map(
        shards, mesh=mesh, in_specs=placed, out_specs=P("chan", "tm"), check_vma=False
    )
```

```python
import functools
import math

import jax
import jax.numpy as jnp
import numpy as np
from jax import lax
from jax.experimental import pallas as pl
from jax.experimental.pallas import tpu as pltpu
from jax.sharding import PartitionSpec as P

RADIUS = 16
BLOCK = 256
STATES = 8
SUMS_COST = 6

low_corner = 0.015
high_corner = 100.0
sample_rate = 500.0
highest = lax.Precision.HIGHEST
VMEM = pltpu.VMEM
ANY = pl.ANY


def section(corner, highpass):
    warped = 2.0 * sample_rate * math.tan(math.pi * corner / sample_rate)
    scaled = warped / (2.0 * sample_rate * math.sqrt(2.0))
    numer_real = 1.0 - scaled
    denom_real = 1.0 + scaled
    denom_imag = -scaled
    modulus = denom_real * denom_real + denom_imag * denom_imag
    pole_real = (numer_real * denom_real + scaled * denom_imag) / modulus
    pole_imag = (scaled * denom_real - numer_real * denom_imag) / modulus
    pole_norm = pole_real * pole_real + pole_imag * pole_imag
    zero_place = 1.0 if highpass else -1.0
    section_gain = ((1.0 + zero_place * pole_real) ** 2 + pole_imag * pole_imag) / 4.0
    linear = section_gain * (2.0 * pole_real - 2.0 * zero_place)
    constant = section_gain * (1.0 - pole_norm)
    shrink = 1.0 - math.sqrt(pole_norm)
    first_out = linear / shrink
    second = (constant + pole_real * linear) / (pole_imag * shrink)
    rotation = np.array([[pole_real, -pole_imag], [pole_imag, pole_real]])
    inject = np.array([shrink, 0.0])
    return (rotation, inject, np.array([first_out, second]), section_gain)


def filter_system():
    high_rotation, high_inject, high_out, high_gain = section(low_corner, True)
    low_rotation, low_inject, low_out, low_gain = section(high_corner, False)
    upper_rows = np.concatenate([high_rotation, np.zeros((2, 2))], axis=1)
    lower_rows = np.concatenate([np.outer(low_inject, high_out), low_rotation], axis=1)
    transition = np.concatenate([upper_rows, lower_rows], axis=0)
    driving = np.concatenate([high_inject, low_inject * high_gain])
    readout = np.concatenate([high_out * low_gain, low_out])
    direct = low_gain * high_gain
    return (transition, driving, readout, direct)


def spatial_taps(extent):
    positions = np.arange(-extent, extent + 1)
    window = 0.5 * (1.0 + np.cos(np.pi * positions / (extent + 1)))
    window = window / np.sum(window)
    return np.where(positions == 0, 1.0 - window, -window)


def two_sided():
    transition, driving, readout, direct = filter_system()
    poles, vectors = np.linalg.eig(transition)
    gains = (readout @ vectors) * (np.linalg.inv(vectors) @ driving)
    pairs = 1.0 / (1.0 - poles[:, None] * poles[None, :])
    rho = direct * gains + gains * poles * (gains @ pairs)
    r0 = (direct * direct + gains @ pairs @ gains).real
    cut = -(gains / rho)[:, None] * pairs * gains[None, :]
    kept = [i for i in range(4) if poles[i].imag > 0]
    twin = [int(np.argmin(abs(poles - np.conj(poles[i])))) for i in kept]
    scale = 1.0 - abs(poles[kept])
    end = np.zeros((4, 4))
    for i, a in enumerate(kept):
        for j, (b, c) in enumerate(zip(kept, twin)):
            straight, crossed = cut[a, b], cut[a, c]
            of_real, of_imag = straight + crossed, 1j * (straight - crossed)
            ratio = scale[i] / scale[j]
            end[2 * i, 2 * j : 2 * j + 2] = of_real.real * ratio, of_imag.real * ratio
            end[2 * i + 1, 2 * j : 2 * j + 2] = of_real.imag * ratio, of_imag.imag * ratio
    return r0, rho[kept], poles[kept], scale, end


def power(poles, steps):
    out = np.zeros((4, 4))
    for i, p in enumerate(poles**steps):
        out[2 * i : 2 * i + 2, 2 * i : 2 * i + 2] = [[p.real, -p.imag], [p.imag, p.real]]
    return out


def met(place, step, parts):
    if parts & (parts - 1) == 0:
        return place ^ step, place ^ step
    return (place + step) % parts, (place - step) % parts


def time_tables(samples, parts):
    r0, rho, poles, scale, end = two_sided()
    blocks = samples // BLOCK
    lanes = blocks * STATES
    k = np.arange(BLOCK)
    r = np.concatenate([[r0], sum(2.0 * (c * p ** k[:-1]).real for c, p in zip(rho, poles))])
    toeplitz = r[abs(k[:, None] - k[None, :])]
    gather = np.zeros((BLOCK, STATES))
    spread = np.zeros((STATES, BLOCK))
    for i, (p, s, c) in enumerate(zip(poles, scale, rho)):
        for side, far, near in ((0, BLOCK - 1 - k, k), (4, k, BLOCK - 1 - k)):
            inject = s * p**far
            out = 2.0 * c / s * p**near
            gather[:, side + 2 * i] = inject.real
            gather[:, side + 2 * i + 1] = inject.imag
            spread[side + 2 * i] = out.real
            spread[side + 2 * i + 1] = -out.imag
    gather = np.tile(gather, (1, blocks))
    spread = np.tile(spread, (blocks, 1))
    step = [power(poles, BLOCK * m).T for m in range(blocks + 1)]
    inner = np.zeros((blocks, STATES, blocks, STATES))
    whole = np.zeros((blocks, STATES, STATES))
    carry = np.zeros((STATES, blocks, STATES))
    for b in range(blocks):
        for c in range(blocks):
            if c < b:
                inner[c, :4, b, :4] = step[b - c - 1]
            if c > b:
                inner[c, 4:, b, 4:] = step[c - b - 1]
        whole[b, :4, :4] = step[blocks - 1 - b]
        whole[b, 4:, 4:] = step[b]
        carry[:4, b, :4] = step[b]
        carry[4:, b, 4:] = step[blocks - 1 - b]
    inner = inner.reshape(lanes, lanes)
    whole = whole.reshape(lanes, STATES).T
    carry = carry.reshape(STATES, lanes)
    device = [power(poles, samples * m).T for m in range(parts + 1)]
    enter = np.zeros((parts, parts * STATES, lanes))
    for t in range(parts):
        for j in range(parts):
            at = met(t, j, parts)[1]
            into = np.zeros((STATES, STATES))
            if at < t:
                into[:4, :4] = device[t - at - 1]
            if at > t:
                into[4:, 4:] = device[at - t - 1]
            into[:4, 4:] = device[parts - 1 - at] @ end.T @ device[parts - 1 - t]
            enter[t, STATES * j : STATES * (j + 1)] = into @ carry
    return [np.asarray(v, np.float32) for v in (toeplitz, gather, spread, inner, whole, enter)]


def mix_tables(channels):
    taps = spatial_taps(RADIUS)

    def between(rows, columns):
        lag = columns[None, :] - rows[:, None]
        return np.where(abs(lag) <= RADIUS, taps[np.clip(lag + RADIUS, 0, 2 * RADIUS)], 0.0)

    mine = np.arange(channels)
    own = between(mine, mine)
    after = between(mine, channels + np.arange(RADIUS))
    before = between(mine, np.arange(-RADIUS, 0))
    both = [np.concatenate(v, axis=1) for v in ((own, after, before), (own, before, after))]
    return np.stack(both).astype(np.float32)


def halves(value):
    value = np.asarray(value, np.float32)
    high = value.astype(jnp.bfloat16)
    return high, (value - high.astype(np.float32)).astype(jnp.bfloat16)


def split(value):
    high = value.astype(jnp.bfloat16)
    return high, (value - high.astype(jnp.float32)).astype(jnp.bfloat16)


def exact(a, b):
    return jnp.dot(a, b, precision=highest, preferred_element_type=jnp.float32)


def product(a, b):
    return jnp.dot(a, b, preferred_element_type=jnp.float32)


def mixing(weights, x):
    a, b = split(weights)
    high, low = split(x)
    return product(jnp.concatenate([a, b, a], axis=1), jnp.concatenate([high, high, low], axis=0))


def filtering(rows, toeplitz):
    high, low = split(rows)
    above, below = toeplitz[:BLOCK], toeplitz[BLOCK:]
    return product(
        jnp.concatenate([high, high, low], axis=1), jnp.concatenate([above, below, above], axis=0)
    )


def place():
    return lax.rem(lax.axis_index("chan"), 2)


def rows_of(x):
    return jnp.concatenate([x[:, i : i + BLOCK] for i in range(0, x.shape[1], BLOCK)], axis=0)


def keep_own(stacked, groups):
    rows = stacked.shape[0] // groups
    owner = lax.broadcasted_iota(jnp.int32, (rows, stacked.shape[1]), 1) // STATES
    return sum(
        jnp.where(owner == g, stacked[g * rows : (g + 1) * rows], 0.0) for g in range(groups)
    )


def spreading(states, groups, spread):
    lanes = states.shape[1]
    owner = lax.broadcasted_iota(jnp.int32, states.shape, 1) // STATES
    high, low = split(
        jnp.concatenate([jnp.where(owner == g, states, 0.0) for g in range(groups)], axis=0)
    )
    above, below = spread[:lanes], spread[lanes:]
    return product(
        jnp.concatenate([high, low, high], axis=1), jnp.concatenate([above, above, below], axis=0)
    )


def start_kernel(cuts, x_hbm, mask_hbm, gather_hbm, *refs):
    first1, second1, first2, second2, live, sums, x, mask, gather, sems = refs
    channels = x.shape[0]
    lanes = sums.shape[1]
    copies = [
        pltpu.make_async_copy(source, target, sems.at[i])
        for i, (source, target) in enumerate([(mask_hbm, mask), (gather_hbm, gather), (x_hbm, x)])
    ]
    for copy in copies:
        copy.start()
    odd = place()
    copies[0].wait()
    same = lax.broadcasted_iota(jnp.int32, (channels, channels), 0) == lax.broadcasted_iota(
        jnp.int32, (channels, channels), 1
    )
    alive = jnp.sum(
        jnp.where(same, mask[...].astype(jnp.float32), 0.0), axis=1, keepdims=True
    )
    copies[1].wait()
    copies[2].wait()
    here = x[...] * alive
    live[...] = here

    def send(value, first, second):
        top, bottom = value[:RADIUS], value[channels - RADIUS :]
        for out, even_rows, odd_rows in ((first, bottom, top), (second, top, bottom)):
            rows = jnp.where(odd == 1, odd_rows, even_rows)
            start = 0
            for ref, at, stop in out:
                if stop > start:
                    ref[:, at : at + stop - start] = rows[:, start:stop]
                start = stop

    samples = here.shape[1]
    send(
        here,
        [(first1, lanes, cuts[0]), (first2, 0, samples)],
        [(second1, lanes, cuts[1]), (second2, 0, samples)],
    )
    high, low = split(rows_of(here))
    wide = product(high, gather[...])
    found = wide[:, :lanes] + wide[:, lanes:] + product(low, gather[:, :lanes])
    total = keep_own(found, samples // BLOCK)
    sums[...] = total
    send(total, [(first1, 0, lanes)], [(second1, 0, lanes)])


def sums_kernel(sums, first1, second1, mix, whole, out, device_out):
    lanes = sums.shape[1]
    stacked = jnp.concatenate([sums[...], first1[:, :lanes], second1[:, :lanes]], axis=0)
    total = exact(mix[place()], stacked)
    out[...] = total
    device_out[...] = lax.dot_general(
        whole[...], total, (((1,), (1,)), ((), ())), precision=highest
    )


def padded(value, before, after):
    rows = value.shape[0]
    sides = [jnp.zeros((rows, n), jnp.float32) if n else None for n in (before, after)]
    return jnp.concatenate([v for v in (sides[0], value, sides[1]) if v is not None], axis=1)


def early_kernel(live, first1, second1, sums, mix, toeplitz, inner, out, states):
    channels, samples = live.shape
    lanes = sums.shape[1]
    states[...] = exact(sums[...], inner[...])
    edges = [padded(ref[:, lanes:], 0, samples + lanes - ref.shape[1]) for ref in (first1, second1)]
    mixed = mixing(mix[place()], jnp.concatenate([live[...], *edges], axis=0))
    rows = filtering(rows_of(mixed), toeplitz[...])
    for b in range(samples // BLOCK):
        out[:, b * BLOCK : (b + 1) * BLOCK] = rows[b * channels : (b + 1) * channels]


def edge_rows(which, edge, mix, toeplitz, channels):
    at = channels + which * RADIUS
    weights = mix[place()][:, at : at + RADIUS]
    return filtering(rows_of(mixing(weights, edge)), toeplitz[...])


def late_kernel(part, second2, mix, toeplitz, out):
    channels, samples = part.shape
    start = samples - second2.shape[1]
    rows = edge_rows(1, second2[...], mix, toeplitz, channels)
    out[:, :start] = part[:, :start]
    for b in range((samples - start) // BLOCK):
        here = slice(start + b * BLOCK, start + (b + 1) * BLOCK)
        out[:, here] = part[:, here] + rows[b * channels : (b + 1) * channels]


def enter_kernel(part, states, enter, spread, *refs):
    devices, out = refs[:-1], refs[-1]
    channels, samples = part.shape
    arrived = jnp.concatenate([ref[...] for ref in devices], axis=0)
    inside = states[...] + lax.dot_general(
        arrived, enter[lax.axis_index("tm")], (((0,), (0,)), ((), ())), precision=highest
    )
    groups = samples // BLOCK
    rows = spreading(inside, groups, spread[...])
    for b in range(groups):
        here = slice(b * BLOCK, (b + 1) * BLOCK)
        out[:, here] = part[:, here] + rows[b * channels : (b + 1) * channels]


def finish_kernel(part, first2, mix, toeplitz, out_hbm, out, sems):
    channels, samples = part.shape
    start = samples - first2.shape[1]
    done = pltpu.make_async_copy(part.at[:, :start], out_hbm.at[:, :start], sems.at[0])
    done.start()
    rows = edge_rows(0, first2[...], mix, toeplitz, channels)
    for b in range((samples - start) // BLOCK):
        here = slice(start + b * BLOCK, start + (b + 1) * BLOCK)
        out[:, b * BLOCK : (b + 1) * BLOCK] = part[:, here] + rows[b * channels : (b + 1) * channels]
    last = pltpu.make_async_copy(out, out_hbm.at[:, start:], sems.at[1])
    last.start()
    done.wait()
    last.wait()


def vmem(*shape, dtype=jnp.float32):
    return pltpu.VMEM(shape, dtype)


def kernel(body, name, inputs, outputs, scratch=(), cost=0, far=()):
    inputs = [
        pltpu.with_memory_space_constraint(v, pltpu.HBM if i in far else VMEM)
        for i, v in enumerate(inputs)
    ]
    out_specs = [
        pl.BlockSpec(memory_space=ANY if isinstance(o, jax.ShapeDtypeStruct) else VMEM)
        for o in outputs
    ]
    single = len(outputs) == 1
    return pl.pallas_call(
        body,
        out_shape=outputs[0] if single else tuple(outputs),
        in_specs=[pl.BlockSpec(memory_space=ANY if i in far else VMEM) for i in range(len(inputs))],
        out_specs=out_specs[0] if single else tuple(out_specs),
        scratch_shapes=list(scratch),
        compiler_params=pltpu.CompilerParams(vmem_limit_bytes=24 * 1024 * 1024),
        cost_estimate=pl.CostEstimate(flops=cost * 100000000, bytes_accessed=0, transcendentals=0),
        name=name,
    )(*inputs)


def shards(strain, channel_mask):
    channels, samples = strain.shape
    parts = lax.axis_size("tm")
    places = lax.axis_size("chan")
    lanes = samples // BLOCK * STATES
    cuts = (samples * 5 // 8 // BLOCK * BLOCK, samples * 3 // 8 // BLOCK * BLOCK)
    toeplitz, gather, spread, inner, whole, enter = time_tables(samples, parts)
    gather = jnp.asarray(np.concatenate(halves(gather), axis=1))
    toeplitz = jnp.asarray(np.concatenate(halves(toeplitz), axis=0))
    spread = jnp.asarray(np.concatenate(halves(spread), axis=0))
    inner, whole, enter = map(jnp.asarray, (inner, whole, enter))
    mix = jnp.asarray(mix_tables(channels))

    pairs = [
        [(i + a, i + b) for i in range(start, places - 1, 2) for a, b in ((0, 1), (1, 0))]
        for start in (0, 1)
    ]
    first1, second1, first2, second2, live, sums = kernel(
        functools.partial(start_kernel, cuts),
        "start",
        [strain, channel_mask.reshape(1, channels), gather],
        [
            vmem(RADIUS, lanes + cuts[0]),
            vmem(RADIUS, lanes + cuts[1]),
            vmem(RADIUS, samples - cuts[0]),
            vmem(RADIUS, samples - cuts[1]),
            vmem(channels, samples),
            vmem(channels, lanes),
        ],
        [
            vmem(channels, samples),
            vmem(1, channels, dtype=jnp.int32),
            vmem(BLOCK, 2 * lanes, dtype=jnp.bfloat16),
            pltpu.SemaphoreType.DMA((3,)),
        ],
        far=(0, 1, 2),
    )
    first1 = lax.ppermute(first1, "chan", pairs[0])
    second1 = lax.ppermute(second1, "chan", pairs[1])
    first2 = lax.ppermute(first2, "chan", pairs[0])
    second2 = lax.ppermute(second2, "chan", pairs[1])
    sums, device = kernel(
        sums_kernel,
        "sums",
        [sums, first1, second1, mix, whole],
        [vmem(channels, lanes), vmem(STATES, channels)],
        cost=SUMS_COST,
    )
    others = [
        lax.ppermute(device, "tm", [(i, met(i, j, parts)[0]) for i in range(parts)])
        for j in range(1, parts)
    ]
    part, states = kernel(
        early_kernel,
        "early",
        [live, first1, second1, sums, mix, toeplitz, inner],
        [vmem(channels, samples), vmem(channels, lanes)],
    )
    part = kernel(late_kernel, "late", [part, second2, mix, toeplitz], [vmem(channels, samples)])
    part = kernel(
        enter_kernel,
        "enter",
        [part, states, enter, spread, device, *others],
        [vmem(channels, samples)],
    )
    return kernel(
        finish_kernel,
        "finish",
        [part, first2, mix, toeplitz],
        [jax.ShapeDtypeStruct((channels, samples), jnp.float32)],
        [vmem(channels, samples - cuts[0]), pltpu.SemaphoreType.DMA((2,))],
    )


def solution(mesh):
    placed = (P("chan", "tm"), P("chan"))
    return jax.shard_map(
        shards, mesh=mesh, in_specs=placed, out_specs=P("chan", "tm"), check_vma=False
    )
```

```python
import functools
import math

import jax
import jax.numpy as jnp
import numpy as np
from jax import lax
from jax.experimental import pallas as pl
from jax.experimental.pallas import tpu as pltpu
from jax.sharding import PartitionSpec as P

RADIUS = 16
BLOCK = 256
STATES = 8
SUMS_COST = 10

low_corner = 0.015
high_corner = 100.0
sample_rate = 500.0
highest = lax.Precision.HIGHEST
VMEM = pltpu.VMEM
ANY = pl.ANY


def section(corner, highpass):
    warped = 2.0 * sample_rate * math.tan(math.pi * corner / sample_rate)
    scaled = warped / (2.0 * sample_rate * math.sqrt(2.0))
    numer_real = 1.0 - scaled
    denom_real = 1.0 + scaled
    denom_imag = -scaled
    modulus = denom_real * denom_real + denom_imag * denom_imag
    pole_real = (numer_real * denom_real + scaled * denom_imag) / modulus
    pole_imag = (scaled * denom_real - numer_real * denom_imag) / modulus
    pole_norm = pole_real * pole_real + pole_imag * pole_imag
    zero_place = 1.0 if highpass else -1.0
    section_gain = ((1.0 + zero_place * pole_real) ** 2 + pole_imag * pole_imag) / 4.0
    linear = section_gain * (2.0 * pole_real - 2.0 * zero_place)
    constant = section_gain * (1.0 - pole_norm)
    shrink = 1.0 - math.sqrt(pole_norm)
    first_out = linear / shrink
    second = (constant + pole_real * linear) / (pole_imag * shrink)
    rotation = np.array([[pole_real, -pole_imag], [pole_imag, pole_real]])
    inject = np.array([shrink, 0.0])
    return (rotation, inject, np.array([first_out, second]), section_gain)


def filter_system():
    high_rotation, high_inject, high_out, high_gain = section(low_corner, True)
    low_rotation, low_inject, low_out, low_gain = section(high_corner, False)
    upper_rows = np.concatenate([high_rotation, np.zeros((2, 2))], axis=1)
    lower_rows = np.concatenate([np.outer(low_inject, high_out), low_rotation], axis=1)
    transition = np.concatenate([upper_rows, lower_rows], axis=0)
    driving = np.concatenate([high_inject, low_inject * high_gain])
    readout = np.concatenate([high_out * low_gain, low_out])
    direct = low_gain * high_gain
    return (transition, driving, readout, direct)


def spatial_taps(extent):
    positions = np.arange(-extent, extent + 1)
    window = 0.5 * (1.0 + np.cos(np.pi * positions / (extent + 1)))
    window = window / np.sum(window)
    return np.where(positions == 0, 1.0 - window, -window)


def two_sided():
    transition, driving, readout, direct = filter_system()
    poles, vectors = np.linalg.eig(transition)
    gains = (readout @ vectors) * (np.linalg.inv(vectors) @ driving)
    pairs = 1.0 / (1.0 - poles[:, None] * poles[None, :])
    rho = direct * gains + gains * poles * (gains @ pairs)
    r0 = (direct * direct + gains @ pairs @ gains).real
    cut = -(gains / rho)[:, None] * pairs * gains[None, :]
    kept = [i for i in range(4) if poles[i].imag > 0]
    twin = [int(np.argmin(abs(poles - np.conj(poles[i])))) for i in kept]
    scale = 1.0 - abs(poles[kept])
    end = np.zeros((4, 4))
    for i, a in enumerate(kept):
        for j, (b, c) in enumerate(zip(kept, twin)):
            straight, crossed = cut[a, b], cut[a, c]
            of_real, of_imag = straight + crossed, 1j * (straight - crossed)
            ratio = scale[i] / scale[j]
            end[2 * i, 2 * j : 2 * j + 2] = of_real.real * ratio, of_imag.real * ratio
            end[2 * i + 1, 2 * j : 2 * j + 2] = of_real.imag * ratio, of_imag.imag * ratio
    return r0, rho[kept], poles[kept], scale, end


def power(poles, steps):
    out = np.zeros((4, 4))
    for i, p in enumerate(poles**steps):
        out[2 * i : 2 * i + 2, 2 * i : 2 * i + 2] = [[p.real, -p.imag], [p.imag, p.real]]
    return out


def met(place, step, parts):
    if parts & (parts - 1) == 0:
        return place ^ step, place ^ step
    return (place + step) % parts, (place - step) % parts


def time_tables(samples, parts):
    r0, rho, poles, scale, end = two_sided()
    blocks = samples // BLOCK
    lanes = blocks * STATES
    k = np.arange(BLOCK)
    r = np.concatenate([[r0], sum(2.0 * (c * p ** k[:-1]).real for c, p in zip(rho, poles))])
    toeplitz = r[abs(k[:, None] - k[None, :])]
    gather = np.zeros((BLOCK, STATES))
    spread = np.zeros((STATES, BLOCK))
    for i, (p, s, c) in enumerate(zip(poles, scale, rho)):
        for side, far, near in ((0, BLOCK - 1 - k, k), (4, k, BLOCK - 1 - k)):
            inject = s * p**far
            out = 2.0 * c / s * p**near
            gather[:, side + 2 * i] = inject.real
            gather[:, side + 2 * i + 1] = inject.imag
            spread[side + 2 * i] = out.real
            spread[side + 2 * i + 1] = -out.imag
    gather = np.tile(gather, (1, blocks))
    spread = np.tile(spread, (blocks, 1))
    step = [power(poles, BLOCK * m).T for m in range(blocks + 1)]
    inner = np.zeros((blocks, STATES, blocks, STATES))
    whole = np.zeros((blocks, STATES, STATES))
    carry = np.zeros((STATES, blocks, STATES))
    for b in range(blocks):
        for c in range(blocks):
            if c < b:
                inner[c, :4, b, :4] = step[b - c - 1]
            if c > b:
                inner[c, 4:, b, 4:] = step[c - b - 1]
        whole[b, :4, :4] = step[blocks - 1 - b]
        whole[b, 4:, 4:] = step[b]
        carry[:4, b, :4] = step[b]
        carry[4:, b, 4:] = step[blocks - 1 - b]
    inner = inner.reshape(lanes, lanes)
    whole = whole.reshape(lanes, STATES).T
    carry = carry.reshape(STATES, lanes)
    device = [power(poles, samples * m).T for m in range(parts + 1)]
    enter = np.zeros((parts, parts * STATES, lanes))
    for t in range(parts):
        for j in range(parts):
            at = met(t, j, parts)[1]
            into = np.zeros((STATES, STATES))
            if at < t:
                into[:4, :4] = device[t - at - 1]
            if at > t:
                into[4:, 4:] = device[at - t - 1]
            into[:4, 4:] = device[parts - 1 - at] @ end.T @ device[parts - 1 - t]
            enter[t, STATES * j : STATES * (j + 1)] = into @ carry
    return [np.asarray(v, np.float32) for v in (toeplitz, gather, spread, inner, whole, enter)]


def mix_tables(channels):
    taps = spatial_taps(RADIUS)

    def between(rows, columns):
        lag = columns[None, :] - rows[:, None]
        return np.where(abs(lag) <= RADIUS, taps[np.clip(lag + RADIUS, 0, 2 * RADIUS)], 0.0)

    mine = np.arange(channels)
    own = between(mine, mine)
    after = between(mine, channels + np.arange(RADIUS))
    before = between(mine, np.arange(-RADIUS, 0))
    both = [np.concatenate(v, axis=1) for v in ((own, after, before), (own, before, after))]
    return np.stack(both).astype(np.float32)


def halves(value):
    value = np.asarray(value, np.float32)
    high = value.astype(jnp.bfloat16)
    return high, (value - high.astype(np.float32)).astype(jnp.bfloat16)


def split(value):
    high = value.astype(jnp.bfloat16)
    return high, (value - high.astype(jnp.float32)).astype(jnp.bfloat16)


def exact(a, b):
    return jnp.dot(a, b, precision=highest, preferred_element_type=jnp.float32)


def product(a, b):
    return jnp.dot(a, b, preferred_element_type=jnp.float32)


def mixing(weights, x):
    a, b = split(weights)
    high, low = split(x)
    return product(jnp.concatenate([a, b, a], axis=1), jnp.concatenate([high, high, low], axis=0))


def filtering(rows, toeplitz):
    high, low = split(rows)
    above, below = toeplitz[:BLOCK], toeplitz[BLOCK:]
    return product(
        jnp.concatenate([high, high, low], axis=1), jnp.concatenate([above, below, above], axis=0)
    )


def place():
    return lax.rem(lax.axis_index("chan"), 2)


def rows_of(x):
    return jnp.concatenate([x[:, i : i + BLOCK] for i in range(0, x.shape[1], BLOCK)], axis=0)


def keep_own(stacked, groups):
    rows = stacked.shape[0] // groups
    owner = lax.broadcasted_iota(jnp.int32, (rows, stacked.shape[1]), 1) // STATES
    return sum(
        jnp.where(owner == g, stacked[g * rows : (g + 1) * rows], 0.0) for g in range(groups)
    )


def turned(a, b):
    a_high, a_low = split(a)
    b_high, b_low = split(b)
    return lax.dot_general(
        jnp.concatenate([a_high, a_low, a_high], axis=0),
        jnp.concatenate([b_high, b_high, b_low], axis=0),
        (((0,), (0,)), ((), ())),
        preferred_element_type=jnp.float32,
    )


def spreading(states, first, groups, spread):
    lanes = states.shape[1]
    owner = lax.broadcasted_iota(jnp.int32, states.shape, 1) // STATES
    high, low = split(
        jnp.concatenate([jnp.where(owner == first + g, states, 0.0) for g in range(groups)], axis=0)
    )
    above, below = spread[:lanes], spread[lanes:]
    return product(
        jnp.concatenate([high, low, high], axis=1), jnp.concatenate([above, above, below], axis=0)
    )


def start_kernel(cuts, x_hbm, mask_hbm, gather_hbm, *refs):
    first1, second1, first2, second2, live, sums, x, mask, gather, sems = refs
    channels = x.shape[0]
    lanes = sums.shape[1]
    copies = [
        pltpu.make_async_copy(source, target, sems.at[i])
        for i, (source, target) in enumerate([(mask_hbm, mask), (gather_hbm, gather), (x_hbm, x)])
    ]
    for copy in copies:
        copy.start()
    odd = place()
    copies[0].wait()
    same = lax.broadcasted_iota(jnp.int32, (channels, channels), 0) == lax.broadcasted_iota(
        jnp.int32, (channels, channels), 1
    )
    alive = jnp.sum(
        jnp.where(same, mask[...].astype(jnp.float32), 0.0), axis=1, keepdims=True
    )
    copies[1].wait()
    copies[2].wait()
    here = x[...] * alive
    live[...] = here

    def send(value, first, second):
        top, bottom = value[:RADIUS], value[channels - RADIUS :]
        for out, even_rows, odd_rows in ((first, bottom, top), (second, top, bottom)):
            rows = jnp.where(odd == 1, odd_rows, even_rows)
            start = 0
            for ref, at, stop in out:
                if stop > start:
                    ref[:, at : at + stop - start] = rows[:, start:stop]
                start = stop

    samples = here.shape[1]
    send(
        here,
        [(first1, lanes, cuts[0]), (first2, 0, samples)],
        [(second1, lanes, cuts[1]), (second2, 0, samples)],
    )
    high, low = split(rows_of(here))
    wide = product(high, gather[...])
    found = wide[:, :lanes] + wide[:, lanes:] + product(low, gather[:, :lanes])
    total = keep_own(found, samples // BLOCK)
    sums[...] = total
    send(total, [(first1, 0, lanes)], [(second1, 0, lanes)])


def sums_kernel(sums, first1, second1, mix, whole, out, device_out):
    lanes = sums.shape[1]
    stacked = jnp.concatenate([sums[...], first1[:, :lanes], second1[:, :lanes]], axis=0)
    total = exact(mix[place()], stacked)
    out[...] = total
    device_out[...] = lax.dot_general(
        whole[...], total, (((1,), (1,)), ((), ())), precision=highest
    )


def padded(value, before, after):
    rows = value.shape[0]
    sides = [jnp.zeros((rows, n), jnp.float32) if n else None for n in (before, after)]
    return jnp.concatenate([v for v in (sides[0], value, sides[1]) if v is not None], axis=1)


def early_kernel(live, first1, second1, sums, mix, toeplitz, inner, enter_hbm, spread_hbm, *refs):
    out, states, enter, spread, sems = refs
    channels, samples = live.shape
    lanes = sums.shape[1]
    copies = [
        pltpu.make_async_copy(enter_hbm.at[lax.axis_index("tm")], enter, sems.at[0]),
        pltpu.make_async_copy(spread_hbm, spread, sems.at[1]),
    ]
    for copy in copies:
        copy.start()
    states[...] = exact(sums[...], inner[...])
    edges = [padded(ref[:, lanes:], 0, samples + lanes - ref.shape[1]) for ref in (first1, second1)]
    mixed = mixing(mix[place()], jnp.concatenate([live[...], *edges], axis=0))
    rows = filtering(rows_of(mixed), toeplitz[...])
    for b in range(samples // BLOCK):
        out[:, b * BLOCK : (b + 1) * BLOCK] = rows[b * channels : (b + 1) * channels]
    for copy in copies:
        copy.wait()


def edge_rows(which, edge, mix, toeplitz, channels):
    at = channels + which * RADIUS
    weights = mix[place()][:, at : at + RADIUS]
    return filtering(rows_of(mixing(weights, edge)), toeplitz[...])


def late_kernel(part, second2, mix, toeplitz, out):
    channels, samples = part.shape
    start = samples - second2.shape[1]
    rows = edge_rows(1, second2[...], mix, toeplitz, channels)
    out[:, :start] = part[:, :start]
    for b in range((samples - start) // BLOCK):
        here = slice(start + b * BLOCK, start + (b + 1) * BLOCK)
        out[:, here] = part[:, here] + rows[b * channels : (b + 1) * channels]


def finish_kernel(pieces, part, states, first2, mix, toeplitz, enter, spread, *refs):
    devices, (out_hbm, out, sems) = refs[:-3], refs[-3:]
    channels, samples = part.shape
    start = samples - first2.shape[1]
    arrived = jnp.concatenate([ref[...] for ref in devices], axis=0)
    inside = states[...] + turned(arrived, enter[...])
    stores = []
    for i, (low, high) in enumerate(pieces):
        groups = (high - low) // BLOCK
        rows = spreading(inside, low // BLOCK, groups, spread[...])
        if low >= start:
            edge = first2[:, low - start : high - start]
            rows += edge_rows(0, edge, mix, toeplitz, channels)
        for b in range(groups):
            here = slice(low + b * BLOCK, low + (b + 1) * BLOCK)
            out[:, here] = part[:, here] + rows[b * channels : (b + 1) * channels]
        p = pl.ds(low, high - low)
        stores.append(pltpu.make_async_copy(out.at[:, p], out_hbm.at[:, p], sems.at[i]))
        stores[-1].start()
    for copy in stores:
        copy.wait()


def vmem(*shape, dtype=jnp.float32):
    return pltpu.VMEM(shape, dtype)


def kernel(body, name, inputs, outputs, scratch=(), cost=0, far=()):
    inputs = [
        pltpu.with_memory_space_constraint(v, pltpu.HBM if i in far else VMEM)
        for i, v in enumerate(inputs)
    ]
    out_specs = [
        pl.BlockSpec(memory_space=ANY if isinstance(o, jax.ShapeDtypeStruct) else VMEM)
        for o in outputs
    ]
    single = len(outputs) == 1
    return pl.pallas_call(
        body,
        out_shape=outputs[0] if single else tuple(outputs),
        in_specs=[pl.BlockSpec(memory_space=ANY if i in far else VMEM) for i in range(len(inputs))],
        out_specs=out_specs[0] if single else tuple(out_specs),
        scratch_shapes=list(scratch),
        compiler_params=pltpu.CompilerParams(vmem_limit_bytes=24 * 1024 * 1024),
        cost_estimate=pl.CostEstimate(flops=cost * 100000000, bytes_accessed=0, transcendentals=0),
        name=name,
    )(*inputs)


def shards(strain, channel_mask):
    channels, samples = strain.shape
    parts = lax.axis_size("tm")
    places = lax.axis_size("chan")
    lanes = samples // BLOCK * STATES
    cuts = (samples * 3 // 4 // BLOCK * BLOCK, samples * 5 // 16 // BLOCK * BLOCK)
    toeplitz, gather, spread, inner, whole, enter = time_tables(samples, parts)
    gather = jnp.asarray(np.concatenate(halves(gather), axis=1))
    toeplitz = jnp.asarray(np.concatenate(halves(toeplitz), axis=0))
    spread = jnp.asarray(np.concatenate(halves(spread), axis=0))
    inner, whole, enter = map(jnp.asarray, (inner, whole, enter))
    mix = jnp.asarray(mix_tables(channels))

    pairs = [
        [(i + a, i + b) for i in range(start, places - 1, 2) for a, b in ((0, 1), (1, 0))]
        for start in (0, 1)
    ]
    first1, second1, first2, second2, live, sums = kernel(
        functools.partial(start_kernel, cuts),
        "start",
        [strain, channel_mask.reshape(1, channels), gather],
        [
            vmem(RADIUS, lanes + cuts[0]),
            vmem(RADIUS, lanes + cuts[1]),
            vmem(RADIUS, samples - cuts[0]),
            vmem(RADIUS, samples - cuts[1]),
            vmem(channels, samples),
            vmem(channels, lanes),
        ],
        [
            vmem(channels, samples),
            vmem(1, channels, dtype=jnp.int32),
            vmem(BLOCK, 2 * lanes, dtype=jnp.bfloat16),
            pltpu.SemaphoreType.DMA((3,)),
        ],
        far=(0, 1, 2),
    )
    first1 = lax.ppermute(first1, "chan", pairs[0])
    second1 = lax.ppermute(second1, "chan", pairs[1])
    first2 = lax.ppermute(first2, "chan", pairs[0])
    second2 = lax.ppermute(second2, "chan", pairs[1])
    sums, device = kernel(
        sums_kernel,
        "sums",
        [sums, first1, second1, mix, whole],
        [vmem(channels, lanes), vmem(STATES, channels)],
        cost=SUMS_COST,
    )
    others = [
        lax.ppermute(device, "tm", [(i, met(i, j, parts)[0]) for i in range(parts)])
        for j in range(1, parts)
    ]
    part, states, enter, spread = kernel(
        early_kernel,
        "early",
        [live, first1, second1, sums, mix, toeplitz, inner, enter, spread],
        [
            vmem(channels, samples),
            vmem(channels, lanes),
            vmem(*enter.shape[1:]),
            vmem(*spread.shape, dtype=jnp.bfloat16),
        ],
        [pltpu.SemaphoreType.DMA((2,))],
        far=(7, 8),
    )
    part = kernel(late_kernel, "late", [part, second2, mix, toeplitz], [vmem(channels, samples)])
    step = max(BLOCK, samples // 4 // BLOCK * BLOCK)
    edges = sorted({cuts[0], samples, *range(0, samples, step)})
    pieces = list(zip(edges[:-1], edges[1:]))[::-1]
    return kernel(
        functools.partial(finish_kernel, pieces),
        "finish",
        [part, states, first2, mix, toeplitz, enter, spread, device, *others],
        [jax.ShapeDtypeStruct((channels, samples), jnp.float32)],
        [vmem(channels, samples), pltpu.SemaphoreType.DMA((len(pieces),))],
    )


def solution(mesh):
    placed = (P("chan", "tm"), P("chan"))
    return jax.shard_map(
        shards, mesh=mesh, in_specs=placed, out_specs=P("chan", "tm"), check_vma=False
    )
```

```python
import functools
import math

import jax
import jax.numpy as jnp
import numpy as np
from jax import lax
from jax.experimental import pallas as pl
from jax.experimental.pallas import tpu as pltpu
from jax.sharding import PartitionSpec as P

RADIUS = 16
BLOCK = 256
STATES = 8
SUMS_COST = 8

low_corner = 0.015
high_corner = 100.0
sample_rate = 500.0
highest = lax.Precision.HIGHEST
VMEM = pltpu.VMEM
ANY = pl.ANY


def section(corner, highpass):
    warped = 2.0 * sample_rate * math.tan(math.pi * corner / sample_rate)
    scaled = warped / (2.0 * sample_rate * math.sqrt(2.0))
    numer_real = 1.0 - scaled
    denom_real = 1.0 + scaled
    denom_imag = -scaled
    modulus = denom_real * denom_real + denom_imag * denom_imag
    pole_real = (numer_real * denom_real + scaled * denom_imag) / modulus
    pole_imag = (scaled * denom_real - numer_real * denom_imag) / modulus
    pole_norm = pole_real * pole_real + pole_imag * pole_imag
    zero_place = 1.0 if highpass else -1.0
    section_gain = ((1.0 + zero_place * pole_real) ** 2 + pole_imag * pole_imag) / 4.0
    linear = section_gain * (2.0 * pole_real - 2.0 * zero_place)
    constant = section_gain * (1.0 - pole_norm)
    shrink = 1.0 - math.sqrt(pole_norm)
    first_out = linear / shrink
    second = (constant + pole_real * linear) / (pole_imag * shrink)
    rotation = np.array([[pole_real, -pole_imag], [pole_imag, pole_real]])
    inject = np.array([shrink, 0.0])
    return (rotation, inject, np.array([first_out, second]), section_gain)


def filter_system():
    high_rotation, high_inject, high_out, high_gain = section(low_corner, True)
    low_rotation, low_inject, low_out, low_gain = section(high_corner, False)
    upper_rows = np.concatenate([high_rotation, np.zeros((2, 2))], axis=1)
    lower_rows = np.concatenate([np.outer(low_inject, high_out), low_rotation], axis=1)
    transition = np.concatenate([upper_rows, lower_rows], axis=0)
    driving = np.concatenate([high_inject, low_inject * high_gain])
    readout = np.concatenate([high_out * low_gain, low_out])
    direct = low_gain * high_gain
    return (transition, driving, readout, direct)


def spatial_taps(extent):
    positions = np.arange(-extent, extent + 1)
    window = 0.5 * (1.0 + np.cos(np.pi * positions / (extent + 1)))
    window = window / np.sum(window)
    return np.where(positions == 0, 1.0 - window, -window)


def two_sided():
    transition, driving, readout, direct = filter_system()
    poles, vectors = np.linalg.eig(transition)
    gains = (readout @ vectors) * (np.linalg.inv(vectors) @ driving)
    pairs = 1.0 / (1.0 - poles[:, None] * poles[None, :])
    rho = direct * gains + gains * poles * (gains @ pairs)
    r0 = (direct * direct + gains @ pairs @ gains).real
    cut = -(gains / rho)[:, None] * pairs * gains[None, :]
    kept = [i for i in range(4) if poles[i].imag > 0]
    twin = [int(np.argmin(abs(poles - np.conj(poles[i])))) for i in kept]
    scale = 1.0 - abs(poles[kept])
    end = np.zeros((4, 4))
    for i, a in enumerate(kept):
        for j, (b, c) in enumerate(zip(kept, twin)):
            straight, crossed = cut[a, b], cut[a, c]
            of_real, of_imag = straight + crossed, 1j * (straight - crossed)
            ratio = scale[i] / scale[j]
            end[2 * i, 2 * j : 2 * j + 2] = of_real.real * ratio, of_imag.real * ratio
            end[2 * i + 1, 2 * j : 2 * j + 2] = of_real.imag * ratio, of_imag.imag * ratio
    return r0, rho[kept], poles[kept], scale, end


def power(poles, steps):
    out = np.zeros((4, 4))
    for i, p in enumerate(poles**steps):
        out[2 * i : 2 * i + 2, 2 * i : 2 * i + 2] = [[p.real, -p.imag], [p.imag, p.real]]
    return out


def met(place, step, parts):
    if parts & (parts - 1) == 0:
        return place ^ step, place ^ step
    return (place + step) % parts, (place - step) % parts


def time_tables(samples, parts):
    r0, rho, poles, scale, end = two_sided()
    blocks = samples // BLOCK
    lanes = blocks * STATES
    k = np.arange(BLOCK)
    r = np.concatenate([[r0], sum(2.0 * (c * p ** k[:-1]).real for c, p in zip(rho, poles))])
    toeplitz = r[abs(k[:, None] - k[None, :])]
    gather = np.zeros((BLOCK, STATES))
    spread = np.zeros((STATES, BLOCK))
    for i, (p, s, c) in enumerate(zip(poles, scale, rho)):
        for side, far, near in ((0, BLOCK - 1 - k, k), (4, k, BLOCK - 1 - k)):
            inject = s * p**far
            out = 2.0 * c / s * p**near
            gather[:, side + 2 * i] = inject.real
            gather[:, side + 2 * i + 1] = inject.imag
            spread[side + 2 * i] = out.real
            spread[side + 2 * i + 1] = -out.imag
    gather = np.tile(gather, (1, blocks))
    spread = np.tile(spread, (blocks, 1))
    step = [power(poles, BLOCK * m).T for m in range(blocks + 1)]
    inner = np.zeros((blocks, STATES, blocks, STATES))
    whole = np.zeros((blocks, STATES, STATES))
    carry = np.zeros((STATES, blocks, STATES))
    for b in range(blocks):
        for c in range(blocks):
            if c < b:
                inner[c, :4, b, :4] = step[b - c - 1]
            if c > b:
                inner[c, 4:, b, 4:] = step[c - b - 1]
        whole[b, :4, :4] = step[blocks - 1 - b]
        whole[b, 4:, 4:] = step[b]
        carry[:4, b, :4] = step[b]
        carry[4:, b, 4:] = step[blocks - 1 - b]
    inner = inner.reshape(lanes, lanes)
    whole = whole.reshape(lanes, STATES).T
    carry = carry.reshape(STATES, lanes)
    device = [power(poles, samples * m).T for m in range(parts + 1)]
    enter = np.zeros((parts, parts * STATES, lanes))
    for t in range(parts):
        for j in range(parts):
            at = met(t, j, parts)[1]
            into = np.zeros((STATES, STATES))
            if at < t:
                into[:4, :4] = device[t - at - 1]
            if at > t:
                into[4:, 4:] = device[at - t - 1]
            into[:4, 4:] = device[parts - 1 - at] @ end.T @ device[parts - 1 - t]
            enter[t, STATES * j : STATES * (j + 1)] = into @ carry
    return [np.asarray(v, np.float32) for v in (toeplitz, gather, spread, inner, whole, enter)]


def mix_tables(channels):
    taps = spatial_taps(RADIUS)

    def between(rows, columns):
        lag = columns[None, :] - rows[:, None]
        return np.where(abs(lag) <= RADIUS, taps[np.clip(lag + RADIUS, 0, 2 * RADIUS)], 0.0)

    mine = np.arange(channels)
    own = between(mine, mine)
    after = between(mine, channels + np.arange(RADIUS))
    before = between(mine, np.arange(-RADIUS, 0))
    both = [np.concatenate(v, axis=1) for v in ((own, after, before), (own, before, after))]
    return np.stack(both).astype(np.float32)


def halves(value):
    value = np.asarray(value, np.float32)
    high = value.astype(jnp.bfloat16)
    return high, (value - high.astype(np.float32)).astype(jnp.bfloat16)


def split(value):
    high = value.astype(jnp.bfloat16)
    return high, (value - high.astype(jnp.float32)).astype(jnp.bfloat16)


def exact(a, b):
    return jnp.dot(a, b, precision=highest, preferred_element_type=jnp.float32)


def product(a, b):
    return jnp.dot(a, b, preferred_element_type=jnp.float32)


def mixing(weights, x):
    a, b = split(weights)
    high, low = split(x)
    return product(jnp.concatenate([a, b, a], axis=1), jnp.concatenate([high, high, low], axis=0))


def filtering(rows, toeplitz):
    high, low = split(rows)
    above, below = toeplitz[:BLOCK], toeplitz[BLOCK:]
    return product(
        jnp.concatenate([high, high, low], axis=1), jnp.concatenate([above, below, above], axis=0)
    )


def place():
    return lax.rem(lax.axis_index("chan"), 2)


def rows_of(x):
    return jnp.concatenate([x[:, i : i + BLOCK] for i in range(0, x.shape[1], BLOCK)], axis=0)


def keep_own(stacked, groups):
    rows = stacked.shape[0] // groups
    owner = lax.broadcasted_iota(jnp.int32, (rows, stacked.shape[1]), 1) // STATES
    return sum(
        jnp.where(owner == g, stacked[g * rows : (g + 1) * rows], 0.0) for g in range(groups)
    )


def turned(a, b):
    a_high, a_low = split(a)
    b_high, b_low = split(b)
    return lax.dot_general(
        jnp.concatenate([a_high, a_low, a_high], axis=0),
        jnp.concatenate([b_high, b_high, b_low], axis=0),
        (((0,), (0,)), ((), ())),
        preferred_element_type=jnp.float32,
    )


def spreading(states, first, groups, spread):
    lanes = states.shape[1]
    owner = lax.broadcasted_iota(jnp.int32, states.shape, 1) // STATES
    high, low = split(
        jnp.concatenate([jnp.where(owner == first + g, states, 0.0) for g in range(groups)], axis=0)
    )
    above, below = spread[:lanes], spread[lanes:]
    return product(
        jnp.concatenate([high, low, high], axis=1), jnp.concatenate([above, above, below], axis=0)
    )


def start_kernel(cuts, x_hbm, mask_hbm, gather_hbm, *refs):
    first1, second1, first2, second2, live, sums, x, mask, gather, sems = refs
    channels = x.shape[0]
    lanes = sums.shape[1]
    copies = [
        pltpu.make_async_copy(source, target, sems.at[i])
        for i, (source, target) in enumerate([(mask_hbm, mask), (gather_hbm, gather), (x_hbm, x)])
    ]
    for copy in copies:
        copy.start()
    odd = place()
    copies[0].wait()
    same = lax.broadcasted_iota(jnp.int32, (channels, channels), 0) == lax.broadcasted_iota(
        jnp.int32, (channels, channels), 1
    )
    alive = jnp.sum(
        jnp.where(same, mask[...].astype(jnp.float32), 0.0), axis=1, keepdims=True
    )
    copies[1].wait()
    copies[2].wait()
    here = x[...] * alive
    live[...] = here

    def send(value, first, second):
        top, bottom = value[:RADIUS], value[channels - RADIUS :]
        for out, even_rows, odd_rows in ((first, bottom, top), (second, top, bottom)):
            rows = jnp.where(odd == 1, odd_rows, even_rows)
            start = 0
            for ref, at, stop in out:
                if stop > start:
                    ref[:, at : at + stop - start] = rows[:, start:stop]
                start = stop

    samples = here.shape[1]
    send(
        here,
        [(first1, lanes, cuts[0]), (first2, 0, samples)],
        [(second1, lanes, cuts[1]), (second2, 0, samples)],
    )
    high, low = split(rows_of(here))
    wide = product(high, gather[...])
    found = wide[:, :lanes] + wide[:, lanes:] + product(low, gather[:, :lanes])
    total = keep_own(found, samples // BLOCK)
    sums[...] = total
    send(total, [(first1, 0, lanes)], [(second1, 0, lanes)])


def sums_kernel(sums, first1, second1, mix, whole, out, device_out):
    lanes = sums.shape[1]
    stacked = jnp.concatenate([sums[...], first1[:, :lanes], second1[:, :lanes]], axis=0)
    total = exact(mix[place()], stacked)
    out[...] = total
    device_out[...] = lax.dot_general(
        whole[...], total, (((1,), (1,)), ((), ())), precision=highest
    )


def padded(value, before, after):
    rows = value.shape[0]
    sides = [jnp.zeros((rows, n), jnp.float32) if n else None for n in (before, after)]
    return jnp.concatenate([v for v in (sides[0], value, sides[1]) if v is not None], axis=1)


def early_kernel(live, first1, second1, sums, mix, toeplitz, inner, enter_hbm, spread_hbm, *refs):
    out, states, enter, spread, sems = refs
    channels, samples = live.shape
    lanes = sums.shape[1]
    copies = [
        pltpu.make_async_copy(enter_hbm.at[lax.axis_index("tm")], enter, sems.at[0]),
        pltpu.make_async_copy(spread_hbm, spread, sems.at[1]),
    ]
    for copy in copies:
        copy.start()
    states[...] = exact(sums[...], inner[...])
    edges = [padded(ref[:, lanes:], 0, samples + lanes - ref.shape[1]) for ref in (first1, second1)]
    mixed = mixing(mix[place()], jnp.concatenate([live[...], *edges], axis=0))
    rows = filtering(rows_of(mixed), toeplitz[...])
    for b in range(samples // BLOCK):
        out[:, b * BLOCK : (b + 1) * BLOCK] = rows[b * channels : (b + 1) * channels]
    for copy in copies:
        copy.wait()


def edge_rows(which, edge, mix, toeplitz, channels):
    at = channels + which * RADIUS
    weights = mix[place()][:, at : at + RADIUS]
    return filtering(rows_of(mixing(weights, edge)), toeplitz[...])


def late_kernel(part, second2, mix, toeplitz, out):
    channels, samples = part.shape
    start = samples - second2.shape[1]
    rows = edge_rows(1, second2[...], mix, toeplitz, channels)
    out[:, :start] = part[:, :start]
    for b in range((samples - start) // BLOCK):
        here = slice(start + b * BLOCK, start + (b + 1) * BLOCK)
        out[:, here] = part[:, here] + rows[b * channels : (b + 1) * channels]


def finish_kernel(pieces, part, states, first2, mix, toeplitz, enter, spread, *refs):
    devices, (out_hbm, out, sems) = refs[:-3], refs[-3:]
    channels, samples = part.shape
    start = samples - first2.shape[1]
    arrived = jnp.concatenate([ref[...] for ref in devices], axis=0)
    inside = states[...] + turned(arrived, enter[...])
    stores = []
    for i, (low, high) in enumerate(pieces):
        groups = (high - low) // BLOCK
        rows = spreading(inside, low // BLOCK, groups, spread[...])
        if low >= start:
            edge = first2[:, low - start : high - start]
            rows += edge_rows(0, edge, mix, toeplitz, channels)
        for b in range(groups):
            here = slice(low + b * BLOCK, low + (b + 1) * BLOCK)
            out[:, here] = part[:, here] + rows[b * channels : (b + 1) * channels]
        p = pl.ds(low, high - low)
        stores.append(pltpu.make_async_copy(out.at[:, p], out_hbm.at[:, p], sems.at[i]))
        stores[-1].start()
    for copy in stores:
        copy.wait()


def vmem(*shape, dtype=jnp.float32):
    return pltpu.VMEM(shape, dtype)


def kernel(body, name, inputs, outputs, scratch=(), cost=0, far=()):
    inputs = [
        pltpu.with_memory_space_constraint(v, pltpu.HBM if i in far else VMEM)
        for i, v in enumerate(inputs)
    ]
    out_specs = [
        pl.BlockSpec(memory_space=ANY if isinstance(o, jax.ShapeDtypeStruct) else VMEM)
        for o in outputs
    ]
    single = len(outputs) == 1
    return pl.pallas_call(
        body,
        out_shape=outputs[0] if single else tuple(outputs),
        in_specs=[pl.BlockSpec(memory_space=ANY if i in far else VMEM) for i in range(len(inputs))],
        out_specs=out_specs[0] if single else tuple(out_specs),
        scratch_shapes=list(scratch),
        compiler_params=pltpu.CompilerParams(vmem_limit_bytes=24 * 1024 * 1024),
        cost_estimate=pl.CostEstimate(flops=cost * 100000000, bytes_accessed=0, transcendentals=0),
        name=name,
    )(*inputs)


def shards(strain, channel_mask):
    channels, samples = strain.shape
    parts = lax.axis_size("tm")
    places = lax.axis_size("chan")
    lanes = samples // BLOCK * STATES
    cuts = (samples * 11 // 16 // BLOCK * BLOCK, samples * 3 // 8 // BLOCK * BLOCK)
    toeplitz, gather, spread, inner, whole, enter = time_tables(samples, parts)
    gather = jnp.asarray(np.concatenate(halves(gather), axis=1))
    toeplitz = jnp.asarray(np.concatenate(halves(toeplitz), axis=0))
    spread = jnp.asarray(np.concatenate(halves(spread), axis=0))
    inner, whole, enter = map(jnp.asarray, (inner, whole, enter))
    mix = jnp.asarray(mix_tables(channels))

    pairs = [
        [(i + a, i + b) for i in range(start, places - 1, 2) for a, b in ((0, 1), (1, 0))]
        for start in (0, 1)
    ]
    first1, second1, first2, second2, live, sums = kernel(
        functools.partial(start_kernel, cuts),
        "start",
        [strain, channel_mask.reshape(1, channels), gather],
        [
            vmem(RADIUS, lanes + cuts[0]),
            vmem(RADIUS, lanes + cuts[1]),
            vmem(RADIUS, samples - cuts[0]),
            vmem(RADIUS, samples - cuts[1]),
            vmem(channels, samples),
            vmem(channels, lanes),
        ],
        [
            vmem(channels, samples),
            vmem(1, channels, dtype=jnp.int32),
            vmem(BLOCK, 2 * lanes, dtype=jnp.bfloat16),
            pltpu.SemaphoreType.DMA((3,)),
        ],
        far=(0, 1, 2),
    )
    first1 = lax.ppermute(first1, "chan", pairs[0])
    second1 = lax.ppermute(second1, "chan", pairs[1])
    first2 = lax.ppermute(first2, "chan", pairs[0])
    second2 = lax.ppermute(second2, "chan", pairs[1])
    sums, device = kernel(
        sums_kernel,
        "sums",
        [sums, first1, second1, mix, whole],
        [vmem(channels, lanes), vmem(STATES, channels)],
        cost=SUMS_COST,
    )
    others = [
        lax.ppermute(device, "tm", [(i, met(i, j, parts)[0]) for i in range(parts)])
        for j in range(1, parts)
    ]
    part, states, enter, spread = kernel(
        early_kernel,
        "early",
        [live, first1, second1, sums, mix, toeplitz, inner, enter, spread],
        [
            vmem(channels, samples),
            vmem(channels, lanes),
            vmem(*enter.shape[1:]),
            vmem(*spread.shape, dtype=jnp.bfloat16),
        ],
        [pltpu.SemaphoreType.DMA((2,))],
        far=(7, 8),
    )
    part = kernel(late_kernel, "late", [part, second2, mix, toeplitz], [vmem(channels, samples)])
    middle = cuts[0] // 2 // BLOCK * BLOCK
    pieces = [(middle, cuts[0]), (cuts[0], samples), (0, middle)]
    return kernel(
        functools.partial(finish_kernel, pieces),
        "finish",
        [part, states, first2, mix, toeplitz, enter, spread, device, *others],
        [jax.ShapeDtypeStruct((channels, samples), jnp.float32)],
        [vmem(channels, samples), pltpu.SemaphoreType.DMA((len(pieces),))],
    )


def solution(mesh):
    placed = (P("chan", "tm"), P("chan"))
    return jax.shard_map(
        shards, mesh=mesh, in_specs=placed, out_specs=P("chan", "tm"), check_vma=False
    )
```

```python
import functools
import math

import jax
import jax.numpy as jnp
import numpy as np
from jax import lax
from jax.experimental import pallas as pl
from jax.experimental.pallas import tpu as pltpu
from jax.sharding import PartitionSpec as P

RADIUS = 16
BLOCK = 256
STATES = 8
SUMS_COST = 8

low_corner = 0.015
high_corner = 100.0
sample_rate = 500.0
highest = lax.Precision.HIGHEST
VMEM = pltpu.VMEM
ANY = pl.ANY


def section(corner, highpass):
    warped = 2.0 * sample_rate * math.tan(math.pi * corner / sample_rate)
    scaled = warped / (2.0 * sample_rate * math.sqrt(2.0))
    numer_real = 1.0 - scaled
    denom_real = 1.0 + scaled
    denom_imag = -scaled
    modulus = denom_real * denom_real + denom_imag * denom_imag
    pole_real = (numer_real * denom_real + scaled * denom_imag) / modulus
    pole_imag = (scaled * denom_real - numer_real * denom_imag) / modulus
    pole_norm = pole_real * pole_real + pole_imag * pole_imag
    zero_place = 1.0 if highpass else -1.0
    section_gain = ((1.0 + zero_place * pole_real) ** 2 + pole_imag * pole_imag) / 4.0
    linear = section_gain * (2.0 * pole_real - 2.0 * zero_place)
    constant = section_gain * (1.0 - pole_norm)
    shrink = 1.0 - math.sqrt(pole_norm)
    first_out = linear / shrink
    second = (constant + pole_real * linear) / (pole_imag * shrink)
    rotation = np.array([[pole_real, -pole_imag], [pole_imag, pole_real]])
    inject = np.array([shrink, 0.0])
    return (rotation, inject, np.array([first_out, second]), section_gain)


def filter_system():
    high_rotation, high_inject, high_out, high_gain = section(low_corner, True)
    low_rotation, low_inject, low_out, low_gain = section(high_corner, False)
    upper_rows = np.concatenate([high_rotation, np.zeros((2, 2))], axis=1)
    lower_rows = np.concatenate([np.outer(low_inject, high_out), low_rotation], axis=1)
    transition = np.concatenate([upper_rows, lower_rows], axis=0)
    driving = np.concatenate([high_inject, low_inject * high_gain])
    readout = np.concatenate([high_out * low_gain, low_out])
    direct = low_gain * high_gain
    return (transition, driving, readout, direct)


def spatial_taps(extent):
    positions = np.arange(-extent, extent + 1)
    window = 0.5 * (1.0 + np.cos(np.pi * positions / (extent + 1)))
    window = window / np.sum(window)
    return np.where(positions == 0, 1.0 - window, -window)


def two_sided():
    transition, driving, readout, direct = filter_system()
    poles, vectors = np.linalg.eig(transition)
    gains = (readout @ vectors) * (np.linalg.inv(vectors) @ driving)
    pairs = 1.0 / (1.0 - poles[:, None] * poles[None, :])
    rho = direct * gains + gains * poles * (gains @ pairs)
    r0 = (direct * direct + gains @ pairs @ gains).real
    cut = -(gains / rho)[:, None] * pairs * gains[None, :]
    kept = [i for i in range(4) if poles[i].imag > 0]
    twin = [int(np.argmin(abs(poles - np.conj(poles[i])))) for i in kept]
    scale = 1.0 - abs(poles[kept])
    end = np.zeros((4, 4))
    for i, a in enumerate(kept):
        for j, (b, c) in enumerate(zip(kept, twin)):
            straight, crossed = cut[a, b], cut[a, c]
            of_real, of_imag = straight + crossed, 1j * (straight - crossed)
            ratio = scale[i] / scale[j]
            end[2 * i, 2 * j : 2 * j + 2] = of_real.real * ratio, of_imag.real * ratio
            end[2 * i + 1, 2 * j : 2 * j + 2] = of_real.imag * ratio, of_imag.imag * ratio
    return r0, rho[kept], poles[kept], scale, end


def power(poles, steps):
    out = np.zeros((4, 4))
    for i, p in enumerate(poles**steps):
        out[2 * i : 2 * i + 2, 2 * i : 2 * i + 2] = [[p.real, -p.imag], [p.imag, p.real]]
    return out


def met(place, step, parts):
    if parts & (parts - 1) == 0:
        return place ^ step, place ^ step
    return (place + step) % parts, (place - step) % parts


def time_tables(samples, parts):
    r0, rho, poles, scale, end = two_sided()
    blocks = samples // BLOCK
    lanes = blocks * STATES
    k = np.arange(BLOCK)
    r = np.concatenate([[r0], sum(2.0 * (c * p ** k[:-1]).real for c, p in zip(rho, poles))])
    toeplitz = r[abs(k[:, None] - k[None, :])]
    gather = np.zeros((BLOCK, STATES))
    spread = np.zeros((STATES, BLOCK))
    for i, (p, s, c) in enumerate(zip(poles, scale, rho)):
        for side, far, near in ((0, BLOCK - 1 - k, k), (4, k, BLOCK - 1 - k)):
            inject = s * p**far
            out = 2.0 * c / s * p**near
            gather[:, side + 2 * i] = inject.real
            gather[:, side + 2 * i + 1] = inject.imag
            spread[side + 2 * i] = out.real
            spread[side + 2 * i + 1] = -out.imag
    gather = np.tile(gather, (1, blocks))
    spread = np.tile(spread, (blocks, 1))
    step = [power(poles, BLOCK * m).T for m in range(blocks + 1)]
    inner = np.zeros((blocks, STATES, blocks, STATES))
    whole = np.zeros((blocks, STATES, STATES))
    carry = np.zeros((STATES, blocks, STATES))
    for b in range(blocks):
        for c in range(blocks):
            if c < b:
                inner[c, :4, b, :4] = step[b - c - 1]
            if c > b:
                inner[c, 4:, b, 4:] = step[c - b - 1]
        whole[b, :4, :4] = step[blocks - 1 - b]
        whole[b, 4:, 4:] = step[b]
        carry[:4, b, :4] = step[b]
        carry[4:, b, 4:] = step[blocks - 1 - b]
    inner = inner.reshape(lanes, lanes)
    whole = whole.reshape(lanes, STATES).T
    carry = carry.reshape(STATES, lanes)
    device = [power(poles, samples * m).T for m in range(parts + 1)]
    enter = np.zeros((parts, parts * STATES, lanes))
    for t in range(parts):
        for j in range(parts):
            at = met(t, j, parts)[1]
            into = np.zeros((STATES, STATES))
            if at < t:
                into[:4, :4] = device[t - at - 1]
            if at > t:
                into[4:, 4:] = device[at - t - 1]
            into[:4, 4:] = device[parts - 1 - at] @ end.T @ device[parts - 1 - t]
            enter[t, STATES * j : STATES * (j + 1)] = into @ carry
    return [np.asarray(v, np.float32) for v in (toeplitz, gather, spread, inner, whole, enter)]


def mix_tables(channels):
    taps = spatial_taps(RADIUS)

    def between(rows, columns):
        lag = columns[None, :] - rows[:, None]
        return np.where(abs(lag) <= RADIUS, taps[np.clip(lag + RADIUS, 0, 2 * RADIUS)], 0.0)

    mine = np.arange(channels)
    own = between(mine, mine)
    after = between(mine, channels + np.arange(RADIUS))
    before = between(mine, np.arange(-RADIUS, 0))
    both = [np.concatenate(v, axis=1) for v in ((own, after, before), (own, before, after))]
    return np.stack(both).astype(np.float32)


def halves(value):
    value = np.asarray(value, np.float32)
    high = value.astype(jnp.bfloat16)
    return high, (value - high.astype(np.float32)).astype(jnp.bfloat16)


def split(value):
    high = value.astype(jnp.bfloat16)
    return high, (value - high.astype(jnp.float32)).astype(jnp.bfloat16)


def exact(a, b):
    return jnp.dot(a, b, precision=highest, preferred_element_type=jnp.float32)


def product(a, b):
    return jnp.dot(a, b, preferred_element_type=jnp.float32)


def mixing(weights, x):
    a, b = split(weights)
    high, low = split(x)
    return product(jnp.concatenate([a, b, a], axis=1), jnp.concatenate([high, high, low], axis=0))


def filtering(rows, toeplitz):
    high, low = split(rows)
    above, below = toeplitz[:BLOCK], toeplitz[BLOCK:]
    return product(
        jnp.concatenate([high, high, low], axis=1), jnp.concatenate([above, below, above], axis=0)
    )


def place():
    return lax.rem(lax.axis_index("chan"), 2)


def rows_of(x):
    return jnp.concatenate([x[:, i : i + BLOCK] for i in range(0, x.shape[1], BLOCK)], axis=0)


def keep_own(stacked, groups):
    rows = stacked.shape[0] // groups
    owner = lax.broadcasted_iota(jnp.int32, (rows, stacked.shape[1]), 1) // STATES
    return sum(
        jnp.where(owner == g, stacked[g * rows : (g + 1) * rows], 0.0) for g in range(groups)
    )


def turned(a, b):
    a_high, a_low = split(a)
    b_high, b_low = split(b)
    return lax.dot_general(
        jnp.concatenate([a_high, a_low, a_high], axis=0),
        jnp.concatenate([b_high, b_high, b_low], axis=0),
        (((0,), (0,)), ((), ())),
        preferred_element_type=jnp.float32,
    )


def spreading(states, first, groups, spread):
    lanes = states.shape[1]
    owner = lax.broadcasted_iota(jnp.int32, states.shape, 1) // STATES
    high, low = split(
        jnp.concatenate([jnp.where(owner == first + g, states, 0.0) for g in range(groups)], axis=0)
    )
    above, below = spread[:lanes], spread[lanes:]
    return product(
        jnp.concatenate([high, low, high], axis=1), jnp.concatenate([above, above, below], axis=0)
    )


def start_kernel(cuts, x_hbm, mask_hbm, gather_hbm, *refs):
    first1, second1, first2, second2, live, sums, x, mask, gather, sems = refs
    channels = x.shape[0]
    lanes = sums.shape[1]
    copies = [
        pltpu.make_async_copy(source, target, sems.at[i])
        for i, (source, target) in enumerate([(mask_hbm, mask), (gather_hbm, gather), (x_hbm, x)])
    ]
    for copy in copies:
        copy.start()
    odd = place()
    copies[0].wait()
    same = lax.broadcasted_iota(jnp.int32, (channels, channels), 0) == lax.broadcasted_iota(
        jnp.int32, (channels, channels), 1
    )
    alive = jnp.sum(
        jnp.where(same, mask[...].astype(jnp.float32), 0.0), axis=1, keepdims=True
    )
    copies[1].wait()
    copies[2].wait()
    here = x[...] * alive
    live[...] = here

    def send(value, first, second):
        top, bottom = value[:RADIUS], value[channels - RADIUS :]
        for out, even_rows, odd_rows in ((first, bottom, top), (second, top, bottom)):
            rows = jnp.where(odd == 1, odd_rows, even_rows)
            start = 0
            for ref, at, stop in out:
                if stop > start:
                    ref[:, at : at + stop - start] = rows[:, start:stop]
                start = stop

    samples = here.shape[1]
    send(
        here,
        [(first1, lanes, cuts[0]), (first2, 0, samples)],
        [(second1, lanes, cuts[1]), (second2, 0, samples)],
    )
    high, low = split(rows_of(here))
    wide = product(high, gather[...])
    found = wide[:, :lanes] + wide[:, lanes:] + product(low, gather[:, :lanes])
    total = keep_own(found, samples // BLOCK)
    sums[...] = total
    send(total, [(first1, 0, lanes)], [(second1, 0, lanes)])


def sums_kernel(sums, first1, second1, mix, whole, out, device_out):
    lanes = sums.shape[1]
    stacked = jnp.concatenate([sums[...], first1[:, :lanes], second1[:, :lanes]], axis=0)
    total = exact(mix[place()], stacked)
    out[...] = total
    device_out[...] = lax.dot_general(
        whole[...], total, (((1,), (1,)), ((), ())), precision=highest
    )


def padded(value, before, after):
    rows = value.shape[0]
    sides = [jnp.zeros((rows, n), jnp.float32) if n else None for n in (before, after)]
    return jnp.concatenate([v for v in (sides[0], value, sides[1]) if v is not None], axis=1)


def early_kernel(live, first1, second1, sums, mix, toeplitz, inner, enter_hbm, spread_hbm, *refs):
    out, states, enter, spread, sems = refs
    channels, samples = live.shape
    lanes = sums.shape[1]
    copies = [
        pltpu.make_async_copy(enter_hbm.at[lax.axis_index("tm")], enter, sems.at[0]),
        pltpu.make_async_copy(spread_hbm, spread, sems.at[1]),
    ]
    for copy in copies:
        copy.start()
    states[...] = exact(sums[...], inner[...])
    edges = [padded(ref[:, lanes:], 0, samples + lanes - ref.shape[1]) for ref in (first1, second1)]
    mixed = mixing(mix[place()], jnp.concatenate([live[...], *edges], axis=0))
    rows = filtering(rows_of(mixed), toeplitz[...])
    for b in range(samples // BLOCK):
        out[:, b * BLOCK : (b + 1) * BLOCK] = rows[b * channels : (b + 1) * channels]
    for copy in copies:
        copy.wait()


def edge_rows(which, edge, mix, toeplitz, channels):
    at = channels + which * RADIUS
    weights = mix[place()][:, at : at + RADIUS]
    return filtering(rows_of(mixing(weights, edge)), toeplitz[...])


def late_kernel(part, second2, mix, toeplitz, out):
    channels, samples = part.shape
    start = samples - second2.shape[1]
    rows = edge_rows(1, second2[...], mix, toeplitz, channels)
    for b in range((samples - start) // BLOCK):
        here = slice(start + b * BLOCK, start + (b + 1) * BLOCK)
        out[:, here] = part[:, here] + rows[b * channels : (b + 1) * channels]


def finish_kernel(pieces, part, states, first2, mix, toeplitz, enter, spread, *refs):
    devices, (out_hbm, out, sems) = refs[:-3], refs[-3:]
    channels, samples = part.shape
    start = samples - first2.shape[1]
    arrived = jnp.concatenate([ref[...] for ref in devices], axis=0)
    inside = states[...] + turned(arrived, enter[...])
    stores = []
    for i, (low, high) in enumerate(pieces):
        groups = (high - low) // BLOCK
        rows = spreading(inside, low // BLOCK, groups, spread[...])
        if low >= start:
            edge = first2[:, low - start : high - start]
            rows += edge_rows(0, edge, mix, toeplitz, channels)
        for b in range(groups):
            here = slice(low + b * BLOCK, low + (b + 1) * BLOCK)
            out[:, here] = part[:, here] + rows[b * channels : (b + 1) * channels]
        p = pl.ds(low, high - low)
        stores.append(pltpu.make_async_copy(out.at[:, p], out_hbm.at[:, p], sems.at[i]))
        stores[-1].start()
    for copy in stores:
        copy.wait()


def vmem(*shape, dtype=jnp.float32):
    return pltpu.VMEM(shape, dtype)


def kernel(body, name, inputs, outputs, scratch=(), cost=0, far=(), aliases={}):
    inputs = [
        pltpu.with_memory_space_constraint(v, pltpu.HBM if i in far else VMEM)
        for i, v in enumerate(inputs)
    ]
    out_specs = [
        pl.BlockSpec(memory_space=ANY if isinstance(o, jax.ShapeDtypeStruct) else VMEM)
        for o in outputs
    ]
    single = len(outputs) == 1
    return pl.pallas_call(
        body,
        out_shape=outputs[0] if single else tuple(outputs),
        in_specs=[pl.BlockSpec(memory_space=ANY if i in far else VMEM) for i in range(len(inputs))],
        out_specs=out_specs[0] if single else tuple(out_specs),
        scratch_shapes=list(scratch),
        compiler_params=pltpu.CompilerParams(vmem_limit_bytes=24 * 1024 * 1024),
        cost_estimate=pl.CostEstimate(flops=cost * 100000000, bytes_accessed=0, transcendentals=0),
        input_output_aliases=aliases,
        name=name,
    )(*inputs)


def shards(strain, channel_mask):
    channels, samples = strain.shape
    parts = lax.axis_size("tm")
    places = lax.axis_size("chan")
    lanes = samples // BLOCK * STATES
    cuts = (samples * 11 // 16 // BLOCK * BLOCK, samples * 3 // 8 // BLOCK * BLOCK)
    toeplitz, gather, spread, inner, whole, enter = time_tables(samples, parts)
    gather = jnp.asarray(np.concatenate(halves(gather), axis=1))
    toeplitz = jnp.asarray(np.concatenate(halves(toeplitz), axis=0))
    spread = jnp.asarray(np.concatenate(halves(spread), axis=0))
    inner, whole, enter = map(jnp.asarray, (inner, whole, enter))
    mix = jnp.asarray(mix_tables(channels))

    pairs = [
        [(i + a, i + b) for i in range(start, places - 1, 2) for a, b in ((0, 1), (1, 0))]
        for start in (0, 1)
    ]
    first1, second1, first2, second2, live, sums = kernel(
        functools.partial(start_kernel, cuts),
        "start",
        [strain, channel_mask.reshape(1, channels), gather],
        [
            vmem(RADIUS, lanes + cuts[0]),
            vmem(RADIUS, lanes + cuts[1]),
            vmem(RADIUS, samples - cuts[0]),
            vmem(RADIUS, samples - cuts[1]),
            vmem(channels, samples),
            vmem(channels, lanes),
        ],
        [
            vmem(channels, samples),
            vmem(1, channels, dtype=jnp.int32),
            vmem(BLOCK, 2 * lanes, dtype=jnp.bfloat16),
            pltpu.SemaphoreType.DMA((3,)),
        ],
        far=(0, 1, 2),
    )
    first1 = lax.ppermute(first1, "chan", pairs[0])
    second1 = lax.ppermute(second1, "chan", pairs[1])
    first2 = lax.ppermute(first2, "chan", pairs[0])
    second2 = lax.ppermute(second2, "chan", pairs[1])
    sums, device = kernel(
        sums_kernel,
        "sums",
        [sums, first1, second1, mix, whole],
        [vmem(channels, lanes), vmem(STATES, channels)],
        cost=SUMS_COST,
    )
    others = [
        lax.ppermute(device, "tm", [(i, met(i, j, parts)[0]) for i in range(parts)])
        for j in range(1, parts)
    ]
    part, states, enter, spread = kernel(
        early_kernel,
        "early",
        [live, first1, second1, sums, mix, toeplitz, inner, enter, spread],
        [
            vmem(channels, samples),
            vmem(channels, lanes),
            vmem(*enter.shape[1:]),
            vmem(*spread.shape, dtype=jnp.bfloat16),
        ],
        [pltpu.SemaphoreType.DMA((2,))],
        far=(7, 8),
    )
    part = kernel(
        late_kernel, "late", [part, second2, mix, toeplitz], [vmem(channels, samples)], aliases={0: 0}
    )
    middle = cuts[0] // 2 // BLOCK * BLOCK
    pieces = [(middle, cuts[0]), (cuts[0], samples), (middle // 2 // BLOCK * BLOCK, middle), (0, middle // 2 // BLOCK * BLOCK)]
    return kernel(
        functools.partial(finish_kernel, pieces),
        "finish",
        [part, states, first2, mix, toeplitz, enter, spread, device, *others],
        [jax.ShapeDtypeStruct((channels, samples), jnp.float32)],
        [vmem(channels, samples), pltpu.SemaphoreType.DMA((len(pieces),))],
    )


def solution(mesh):
    placed = (P("chan", "tm"), P("chan"))
    return jax.shard_map(
        shards, mesh=mesh, in_specs=placed, out_specs=P("chan", "tm"), check_vma=False
    )
```

```python
import functools
import math

import jax
import jax.numpy as jnp
import numpy as np
from jax import lax
from jax.experimental import pallas as pl
from jax.experimental.pallas import tpu as pltpu
from jax.sharding import PartitionSpec as P

RADIUS = 16
BLOCK = 256
STATES = 8
SUMS_COST = 8

low_corner = 0.015
high_corner = 100.0
sample_rate = 500.0
highest = lax.Precision.HIGHEST
VMEM = pltpu.VMEM
ANY = pl.ANY


def section(corner, highpass):
    warped = 2.0 * sample_rate * math.tan(math.pi * corner / sample_rate)
    scaled = warped / (2.0 * sample_rate * math.sqrt(2.0))
    numer_real = 1.0 - scaled
    denom_real = 1.0 + scaled
    denom_imag = -scaled
    modulus = denom_real * denom_real + denom_imag * denom_imag
    pole_real = (numer_real * denom_real + scaled * denom_imag) / modulus
    pole_imag = (scaled * denom_real - numer_real * denom_imag) / modulus
    pole_norm = pole_real * pole_real + pole_imag * pole_imag
    zero_place = 1.0 if highpass else -1.0
    section_gain = ((1.0 + zero_place * pole_real) ** 2 + pole_imag * pole_imag) / 4.0
    linear = section_gain * (2.0 * pole_real - 2.0 * zero_place)
    constant = section_gain * (1.0 - pole_norm)
    shrink = 1.0 - math.sqrt(pole_norm)
    first_out = linear / shrink
    second = (constant + pole_real * linear) / (pole_imag * shrink)
    rotation = np.array([[pole_real, -pole_imag], [pole_imag, pole_real]])
    inject = np.array([shrink, 0.0])
    return (rotation, inject, np.array([first_out, second]), section_gain)


def filter_system():
    high_rotation, high_inject, high_out, high_gain = section(low_corner, True)
    low_rotation, low_inject, low_out, low_gain = section(high_corner, False)
    upper_rows = np.concatenate([high_rotation, np.zeros((2, 2))], axis=1)
    lower_rows = np.concatenate([np.outer(low_inject, high_out), low_rotation], axis=1)
    transition = np.concatenate([upper_rows, lower_rows], axis=0)
    driving = np.concatenate([high_inject, low_inject * high_gain])
    readout = np.concatenate([high_out * low_gain, low_out])
    direct = low_gain * high_gain
    return (transition, driving, readout, direct)


def spatial_taps(extent):
    positions = np.arange(-extent, extent + 1)
    window = 0.5 * (1.0 + np.cos(np.pi * positions / (extent + 1)))
    window = window / np.sum(window)
    return np.where(positions == 0, 1.0 - window, -window)


def two_sided():
    transition, driving, readout, direct = filter_system()
    poles, vectors = np.linalg.eig(transition)
    gains = (readout @ vectors) * (np.linalg.inv(vectors) @ driving)
    pairs = 1.0 / (1.0 - poles[:, None] * poles[None, :])
    rho = direct * gains + gains * poles * (gains @ pairs)
    r0 = (direct * direct + gains @ pairs @ gains).real
    cut = -(gains / rho)[:, None] * pairs * gains[None, :]
    kept = [i for i in range(4) if poles[i].imag > 0]
    twin = [int(np.argmin(abs(poles - np.conj(poles[i])))) for i in kept]
    scale = 1.0 - abs(poles[kept])
    end = np.zeros((4, 4))
    for i, a in enumerate(kept):
        for j, (b, c) in enumerate(zip(kept, twin)):
            straight, crossed = cut[a, b], cut[a, c]
            of_real, of_imag = straight + crossed, 1j * (straight - crossed)
            ratio = scale[i] / scale[j]
            end[2 * i, 2 * j : 2 * j + 2] = of_real.real * ratio, of_imag.real * ratio
            end[2 * i + 1, 2 * j : 2 * j + 2] = of_real.imag * ratio, of_imag.imag * ratio
    return r0, rho[kept], poles[kept], scale, end


def power(poles, steps):
    out = np.zeros((4, 4))
    for i, p in enumerate(poles**steps):
        out[2 * i : 2 * i + 2, 2 * i : 2 * i + 2] = [[p.real, -p.imag], [p.imag, p.real]]
    return out


def met(place, step, parts):
    if parts & (parts - 1) == 0:
        return place ^ step, place ^ step
    return (place + step) % parts, (place - step) % parts


def time_tables(samples, parts):
    r0, rho, poles, scale, end = two_sided()
    blocks = samples // BLOCK
    lanes = blocks * STATES
    k = np.arange(BLOCK)
    r = np.concatenate([[r0], sum(2.0 * (c * p ** k[:-1]).real for c, p in zip(rho, poles))])
    toeplitz = r[abs(k[:, None] - k[None, :])]
    gather = np.zeros((BLOCK, STATES))
    spread = np.zeros((STATES, BLOCK))
    for i, (p, s, c) in enumerate(zip(poles, scale, rho)):
        for side, far, near in ((0, BLOCK - 1 - k, k), (4, k, BLOCK - 1 - k)):
            inject = s * p**far
            out = 2.0 * c / s * p**near
            gather[:, side + 2 * i] = inject.real
            gather[:, side + 2 * i + 1] = inject.imag
            spread[side + 2 * i] = out.real
            spread[side + 2 * i + 1] = -out.imag
    gather = np.tile(gather, (1, blocks))
    spread = np.tile(spread, (blocks, 1))
    step = [power(poles, BLOCK * m).T for m in range(blocks + 1)]
    inner = np.zeros((blocks, STATES, blocks, STATES))
    whole = np.zeros((blocks, STATES, STATES))
    carry = np.zeros((STATES, blocks, STATES))
    for b in range(blocks):
        for c in range(blocks):
            if c < b:
                inner[c, :4, b, :4] = step[b - c - 1]
            if c > b:
                inner[c, 4:, b, 4:] = step[c - b - 1]
        whole[b, :4, :4] = step[blocks - 1 - b]
        whole[b, 4:, 4:] = step[b]
        carry[:4, b, :4] = step[b]
        carry[4:, b, 4:] = step[blocks - 1 - b]
    inner = inner.reshape(lanes, lanes)
    whole = whole.reshape(lanes, STATES).T
    carry = carry.reshape(STATES, lanes)
    device = [power(poles, samples * m).T for m in range(parts + 1)]
    enter = np.zeros((parts, parts * STATES, lanes))
    for t in range(parts):
        for j in range(parts):
            at = met(t, j, parts)[1]
            into = np.zeros((STATES, STATES))
            if at < t:
                into[:4, :4] = device[t - at - 1]
            if at > t:
                into[4:, 4:] = device[at - t - 1]
            into[:4, 4:] = device[parts - 1 - at] @ end.T @ device[parts - 1 - t]
            enter[t, STATES * j : STATES * (j + 1)] = into @ carry
    return [np.asarray(v, np.float32) for v in (toeplitz, gather, spread, inner, whole, enter)]


def mix_tables(channels):
    taps = spatial_taps(RADIUS)

    def between(rows, columns):
        lag = columns[None, :] - rows[:, None]
        return np.where(abs(lag) <= RADIUS, taps[np.clip(lag + RADIUS, 0, 2 * RADIUS)], 0.0)

    mine = np.arange(channels)
    own = between(mine, mine)
    after = between(mine, channels + np.arange(RADIUS))
    before = between(mine, np.arange(-RADIUS, 0))
    both = [np.concatenate(v, axis=1) for v in ((own, after, before), (own, before, after))]
    return np.stack(both).astype(np.float32)


def halves(value):
    value = np.asarray(value, np.float32)
    high = value.astype(jnp.bfloat16)
    return high, (value - high.astype(np.float32)).astype(jnp.bfloat16)


def split(value):
    high = value.astype(jnp.bfloat16)
    return high, (value - high.astype(jnp.float32)).astype(jnp.bfloat16)


def exact(a, b):
    return jnp.dot(a, b, precision=highest, preferred_element_type=jnp.float32)


def product(a, b):
    return jnp.dot(a, b, preferred_element_type=jnp.float32)


def mixing(weights, x):
    a, b = split(weights)
    high, low = split(x)
    return product(jnp.concatenate([a, b, a], axis=1), jnp.concatenate([high, high, low], axis=0))


def filtering(rows, toeplitz):
    high, low = split(rows)
    above, below = toeplitz[:BLOCK], toeplitz[BLOCK:]
    return product(
        jnp.concatenate([high, high, low], axis=1), jnp.concatenate([above, below, above], axis=0)
    )


def place():
    return lax.rem(lax.axis_index("chan"), 2)


def rows_of(x):
    return jnp.concatenate([x[:, i : i + BLOCK] for i in range(0, x.shape[1], BLOCK)], axis=0)


def keep_own(stacked, groups):
    rows = stacked.shape[0] // groups
    owner = lax.broadcasted_iota(jnp.int32, (rows, stacked.shape[1]), 1) // STATES
    return sum(
        jnp.where(owner == g, stacked[g * rows : (g + 1) * rows], 0.0) for g in range(groups)
    )


def turned(a, b):
    a_high, a_low = split(a)
    b_high, b_low = split(b)
    return lax.dot_general(
        jnp.concatenate([a_high, a_low, a_high], axis=0),
        jnp.concatenate([b_high, b_high, b_low], axis=0),
        (((0,), (0,)), ((), ())),
        preferred_element_type=jnp.float32,
    )


def spreading(states, first, groups, spread):
    lanes = states.shape[1]
    owner = lax.broadcasted_iota(jnp.int32, states.shape, 1) // STATES
    high, low = split(
        jnp.concatenate([jnp.where(owner == first + g, states, 0.0) for g in range(groups)], axis=0)
    )
    above, below = spread[:lanes], spread[lanes:]
    return product(
        jnp.concatenate([high, low, high], axis=1), jnp.concatenate([above, above, below], axis=0)
    )


def start_kernel(cuts, x_hbm, mask_hbm, gather_hbm, *refs):
    first1, second1, first2, second2, live, sums, x, mask, gather, sems = refs
    channels = x.shape[0]
    lanes = sums.shape[1]
    copies = [
        pltpu.make_async_copy(source, target, sems.at[i])
        for i, (source, target) in enumerate([(mask_hbm, mask), (gather_hbm, gather), (x_hbm, x)])
    ]
    for copy in copies:
        copy.start()
    odd = place()
    copies[0].wait()
    same = lax.broadcasted_iota(jnp.int32, (channels, channels), 0) == lax.broadcasted_iota(
        jnp.int32, (channels, channels), 1
    )
    alive = jnp.sum(
        jnp.where(same, mask[...].astype(jnp.float32), 0.0), axis=1, keepdims=True
    )
    copies[1].wait()
    copies[2].wait()
    here = x[...] * alive
    live[...] = here

    def send(value, first, second):
        top, bottom = value[:RADIUS], value[channels - RADIUS :]
        for out, even_rows, odd_rows in ((first, bottom, top), (second, top, bottom)):
            rows = jnp.where(odd == 1, odd_rows, even_rows)
            start = 0
            for ref, at, stop in out:
                if stop > start:
                    ref[:, at : at + stop - start] = rows[:, start:stop]
                start = stop

    samples = here.shape[1]
    send(
        here,
        [(first1, lanes, cuts[0]), (first2, 0, samples)],
        [(second1, lanes, cuts[1]), (second2, 0, samples)],
    )
    high, low = split(rows_of(here))
    wide = product(high, gather[...])
    found = wide[:, :lanes] + wide[:, lanes:] + product(low, gather[:, :lanes])
    total = keep_own(found, samples // BLOCK)
    sums[...] = total
    send(total, [(first1, 0, lanes)], [(second1, 0, lanes)])


def sums_kernel(sums, first1, second1, mix, whole, out, device_out):
    lanes = sums.shape[1]
    stacked = jnp.concatenate([sums[...], first1[:, :lanes], second1[:, :lanes]], axis=0)
    total = exact(mix[place()], stacked)
    out[...] = total
    device_out[...] = lax.dot_general(
        whole[...], total, (((1,), (1,)), ((), ())), precision=highest
    )


def padded(value, before, after):
    rows = value.shape[0]
    sides = [jnp.zeros((rows, n), jnp.float32) if n else None for n in (before, after)]
    return jnp.concatenate([v for v in (sides[0], value, sides[1]) if v is not None], axis=1)


def early_kernel(live, first1, second1, sums, mix, toeplitz, inner, enter_hbm, spread_hbm, *refs):
    out, states, enter, spread, sems = refs
    channels, samples = live.shape
    lanes = sums.shape[1]
    copies = [
        pltpu.make_async_copy(enter_hbm.at[lax.axis_index("tm")], enter, sems.at[0]),
        pltpu.make_async_copy(spread_hbm, spread, sems.at[1]),
    ]
    for copy in copies:
        copy.start()
    states[...] = exact(sums[...], inner[...])
    edges = [padded(ref[:, lanes:], 0, samples + lanes - ref.shape[1]) for ref in (first1, second1)]
    mixed = mixing(mix[place()], jnp.concatenate([live[...], *edges], axis=0))
    rows = filtering(rows_of(mixed), toeplitz[...])
    for b in range(samples // BLOCK):
        out[:, b * BLOCK : (b + 1) * BLOCK] = rows[b * channels : (b + 1) * channels]
    for copy in copies:
        copy.wait()


def edge_rows(which, edge, mix, toeplitz, channels):
    at = channels + which * RADIUS
    weights = mix[place()][:, at : at + RADIUS]
    return filtering(rows_of(mixing(weights, edge)), toeplitz[...])


def late_kernel(part, second2, mix, toeplitz, out):
    channels, samples = part.shape
    start = samples - second2.shape[1]
    rows = edge_rows(1, second2[...], mix, toeplitz, channels)
    for b in range((samples - start) // BLOCK):
        here = slice(start + b * BLOCK, start + (b + 1) * BLOCK)
        out[:, here] = part[:, here] + rows[b * channels : (b + 1) * channels]


def finish_kernel(pieces, part, states, first2, mix, toeplitz, enter, spread, *refs):
    devices, (out_hbm, out, sems) = refs[:-3], refs[-3:]
    channels, samples = part.shape
    start = samples - first2.shape[1]
    arrived = jnp.concatenate([ref[...] for ref in devices], axis=0)
    inside = states[...] + turned(arrived, enter[...])
    stores = []
    for i, (low, high) in enumerate(pieces):
        groups = (high - low) // BLOCK
        rows = spreading(inside, low // BLOCK, groups, spread[...])
        if low >= start:
            edge = first2[:, low - start : high - start]
            rows += edge_rows(0, edge, mix, toeplitz, channels)
        for b in range(groups):
            here = slice(low + b * BLOCK, low + (b + 1) * BLOCK)
            out[:, here] = part[:, here] + rows[b * channels : (b + 1) * channels]
        p = pl.ds(low, high - low)
        stores.append(pltpu.make_async_copy(out.at[:, p], out_hbm.at[:, p], sems.at[i]))
        stores[-1].start()
    for copy in stores:
        copy.wait()


def vmem(*shape, dtype=jnp.float32):
    return pltpu.VMEM(shape, dtype)


def kernel(body, name, inputs, outputs, scratch=(), cost=0, far=(), aliases={}):
    inputs = [
        pltpu.with_memory_space_constraint(v, pltpu.HBM if i in far else VMEM)
        for i, v in enumerate(inputs)
    ]
    out_specs = [
        pl.BlockSpec(memory_space=ANY if isinstance(o, jax.ShapeDtypeStruct) else VMEM)
        for o in outputs
    ]
    single = len(outputs) == 1
    return pl.pallas_call(
        body,
        out_shape=outputs[0] if single else tuple(outputs),
        in_specs=[pl.BlockSpec(memory_space=ANY if i in far else VMEM) for i in range(len(inputs))],
        out_specs=out_specs[0] if single else tuple(out_specs),
        scratch_shapes=list(scratch),
        compiler_params=pltpu.CompilerParams(vmem_limit_bytes=24 * 1024 * 1024),
        cost_estimate=pl.CostEstimate(flops=cost * 100000000, bytes_accessed=0, transcendentals=0),
        input_output_aliases=aliases,
        name=name,
    )(*inputs)


def shards(strain, channel_mask):
    channels, samples = strain.shape
    parts = lax.axis_size("tm")
    places = lax.axis_size("chan")
    lanes = samples // BLOCK * STATES
    cuts = (samples * 11 // 16 // BLOCK * BLOCK, samples * 7 // 16 // BLOCK * BLOCK)
    toeplitz, gather, spread, inner, whole, enter = time_tables(samples, parts)
    gather = jnp.asarray(np.concatenate(halves(gather), axis=1))
    toeplitz = jnp.asarray(np.concatenate(halves(toeplitz), axis=0))
    spread = jnp.asarray(np.concatenate(halves(spread), axis=0))
    inner, whole, enter = map(jnp.asarray, (inner, whole, enter))
    mix = jnp.asarray(mix_tables(channels))

    pairs = [
        [(i + a, i + b) for i in range(start, places - 1, 2) for a, b in ((0, 1), (1, 0))]
        for start in (0, 1)
    ]
    first1, second1, first2, second2, live, sums = kernel(
        functools.partial(start_kernel, cuts),
        "start",
        [strain, channel_mask.reshape(1, channels), gather],
        [
            vmem(RADIUS, lanes + cuts[0]),
            vmem(RADIUS, lanes + cuts[1]),
            vmem(RADIUS, samples - cuts[0]),
            vmem(RADIUS, samples - cuts[1]),
            vmem(channels, samples),
            vmem(channels, lanes),
        ],
        [
            vmem(channels, samples),
            vmem(1, channels, dtype=jnp.int32),
            vmem(BLOCK, 2 * lanes, dtype=jnp.bfloat16),
            pltpu.SemaphoreType.DMA((3,)),
        ],
        far=(0, 1, 2),
    )
    first1 = lax.ppermute(first1, "chan", pairs[0])
    second1 = lax.ppermute(second1, "chan", pairs[1])
    first2 = lax.ppermute(first2, "chan", pairs[0])
    second2 = lax.ppermute(second2, "chan", pairs[1])
    sums, device = kernel(
        sums_kernel,
        "sums",
        [sums, first1, second1, mix, whole],
        [vmem(channels, lanes), vmem(STATES, channels)],
        cost=SUMS_COST,
    )
    others = [
        lax.ppermute(device, "tm", [(i, met(i, j, parts)[0]) for i in range(parts)])
        for j in range(1, parts)
    ]
    part, states, enter, spread = kernel(
        early_kernel,
        "early",
        [live, first1, second1, sums, mix, toeplitz, inner, enter, spread],
        [
            vmem(channels, samples),
            vmem(channels, lanes),
            vmem(*enter.shape[1:]),
            vmem(*spread.shape, dtype=jnp.bfloat16),
        ],
        [pltpu.SemaphoreType.DMA((2,))],
        far=(7, 8),
    )
    part = kernel(
        late_kernel, "late", [part, second2, mix, toeplitz], [vmem(channels, samples)], aliases={0: 0}
    )
    middle = cuts[0] // 2 // BLOCK * BLOCK
    pieces = [(middle, cuts[0]), (cuts[0], samples), (middle // 2 // BLOCK * BLOCK, middle), (0, middle // 2 // BLOCK * BLOCK)]
    return kernel(
        functools.partial(finish_kernel, pieces),
        "finish",
        [part, states, first2, mix, toeplitz, enter, spread, device, *others],
        [jax.ShapeDtypeStruct((channels, samples), jnp.float32)],
        [vmem(channels, samples), pltpu.SemaphoreType.DMA((len(pieces),))],
    )


def solution(mesh):
    placed = (P("chan", "tm"), P("chan"))
    return jax.shard_map(
        shards, mesh=mesh, in_specs=placed, out_specs=P("chan", "tm"), check_vma=False
    )
```
